32 devices in a mesh: row: 4 (over z), col: 4 (over y, x), section: 2 (over core).
Axes of the slice: x: 2, y: 2, z: 4, core: 2. Of those that a mesh axis runs over, the one named last changes fastest.
Arguments:
- hidden_in: bfloat16 [512, 8192], P(('col', 'section'), 'row'), may hold values from -6 to 6
- norm_gain: float32 [8192], P('row'), may hold values from 0.2 to 4
- gate_weight: bfloat16 [8192, 14336], P('row', ('col', 'section')), may hold values from -0.0625 to 0.0625
- up_weight: bfloat16 [8192, 14336], P('row', ('col', 'section')), may hold values from -0.0625 to 0.0625
- down_weight: bfloat16 [14336, 8192], P(('col', 'section'), 'row'), may hold values from -0.046875 to 0.046875
- proj_weight: bfloat16 [8192, 16384], P('row', ('col', 'section')), may hold values from -0.0625 to 0.0625
- teacher_out: bfloat16 [512, 16384], P(('row', 'col', 'section')), may hold values from -16 to 16
- loss_mask: int32 [512], P('row'), may hold values from 0 to 1, as said below
Outputs:
- loss_value: float32 [], replicated
- grad_gain: float32 [8192], P('row')
- grad_gate: float32 [8192, 14336], P('row', ('col', 'section'))
- grad_up: float32 [8192, 14336], P('row', ('col', 'section'))
- grad_down: float32 [14336, 8192], P(('col', 'section'), 'row')
- grad_proj: float32 [8192, 16384], P('row', ('col', 'section'))
- grad_input: float32 [512, 8192], P(('col', 'section'), 'row')
The draws below stay inside these ranges and needn't reach their ends.
Inputs may be any that keep to these rules, and one draw needn't show every extreme that they name: `loss_mask`: the last token is always kept.
All inputs are finite; a program needn't handle non-finite values.
Results may differ from the reference program's by a relative error of at most 0.033.
Values may be sent and summed in bfloat16 or wider, within the bound.
No kernel may reach another device: no remote copies, remote signals or barrier semaphores. Data moves between devices by JAX's collectives and lax.ppermute only.
A program may use at most 192 MiB of HBM per device.

```python
import jax
import jax.numpy as jnp
from jax import lax

D = 8192
FH = 14336
E = 16384
TOKENS = 512
N_ROW = 4
N_COL = 4
N_SECTION = 2


def draw_loss_mask(key, part):
    position = jnp.arange(TOKENS, dtype=jnp.int32)
    ticket = jax.random.randint(key, (TOKENS,), 0, 1000, dtype=jnp.int32)
    keep = (ticket < 250 + 750 * position // TOKENS).astype(jnp.int32)
    return jnp.where(position == TOKENS - 1, 1, keep).astype(jnp.int32)


def draw_teacher_out(key, part):
    token_frac = (jnp.arange(TOKENS, dtype=jnp.float32) / TOKENS)[:, None]
    feature_frac = (jnp.arange(E, dtype=jnp.float32) / E)[None, :]
    values = jnp.clip(jax.random.normal(key, (TOKENS, E), jnp.float32), -4.0, 4.0)
    scale = (0.4 + 1.6 * token_frac) * (0.6 + 0.8 * feature_frac)
    return (values * scale).astype(jnp.bfloat16)


def draw_norm_gain(key, part):
    feature_frac = jnp.arange(D, dtype=jnp.float32) / D
    subkey = jax.random.fold_in(key, 7)
    rough = jax.random.uniform(subkey, (D,), jnp.float32, 0.75, 1.3)
    base = 0.4 * jnp.exp(feature_frac * jnp.log(6.0))
    return (base * rough).astype(jnp.float32)


def shard_levels(key, shape, split, low, top_value):
    factor_of, own = 1.0, jax.random.fold_in(key, 6)
    for axis_at, blocks in split:
        steps = jnp.exp(jax.random.uniform(jax.random.fold_in(own, axis_at), (blocks,), jnp.float32, low / len(split), top_value / len(split)))
        factor_of = factor_of * jnp.repeat(steps, shape[axis_at] // blocks).reshape([-1 if axis == axis_at else 1 for axis in range(len(shape))])
    return factor_of


def normal_values(rng, shape, spread, reach, pieces=(), held_as=jnp.bfloat16):
    entries = jax.random.normal(rng, shape, jnp.float32) * spread
    if len(pieces) > 0:
        entries = shard_levels(rng, shape, pieces, -0.22, 0.18) * entries
    return jnp.clip(entries, min=-reach, max=reach).astype(held_as)


def setup_inputs(seed: int = 0) -> dict:
    splits = jax.random.split(jax.random.key(seed), 9)
    return {
        "hidden_in": normal_values(splits[0], (TOKENS, D), 1.0, 6.0, ((0, 8), (1, 4))),
        "norm_gain": draw_norm_gain(jax.random.fold_in(splits[8], 71), 0),
        "gate_weight": normal_values(splits[2], (D, FH), D ** -0.5, 0.0625, ((0, 4), (1, 8))),
        "up_weight": normal_values(splits[3], (D, FH), D ** -0.5, 0.0625, ((0, 4), (1, 8))),
        "down_weight": normal_values(splits[4], (FH, D), FH ** -0.5, 0.046875, ((0, 8), (1, 4))),
        "proj_weight": normal_values(splits[5], (D, E), D ** -0.5, 0.0625, ((0, 4), (1, 8))),
        "teacher_out": draw_teacher_out(jax.random.fold_in(splits[8], 71), 0),
        "loss_mask": draw_loss_mask(jax.random.fold_in(splits[8], 71), 0),
    }


def blocked(pairs, parts):
    first_left = pairs[0][0]
    block_size = first_left.shape[1] // parts
    row_count = first_left.shape[0]
    col_count = pairs[0][1].shape[1]

    def advance(running, index):
        partial_value = jnp.zeros((row_count, col_count), jnp.float32)
        for left, right in pairs:
            left_block = lax.dynamic_slice_in_dim(left, index * block_size, block_size, 1)
            right_block = lax.dynamic_slice_in_dim(right, index * block_size, block_size, 0)
            partial_value = partial_value + jnp.dot(left_block, right_block, preferred_element_type=jnp.float32)
        rounded = lax.optimization_barrier(partial_value.astype(jnp.bfloat16))
        return (running + rounded.astype(jnp.float32), None)
    total, unused = lax.scan(advance, jnp.zeros((row_count, col_count), jnp.float32), jnp.arange(parts, dtype=jnp.int32))
    return total

def contract_rows(left, right):
    return lax.dot_general(left, right, (((0,), (0,)), ((), ())), preferred_element_type=jnp.float32)

def silu_parts(gate_val):
    sigma = jax.nn.sigmoid(gate_val)
    return (gate_val * sigma, sigma)

def reference(hidden_in, norm_gain, gate_weight, up_weight, down_weight, proj_weight, teacher_out, loss_mask):
    col_parts = N_COL * N_SECTION
    inputs = hidden_in.astype(jnp.float32)
    inv_rms = lax.rsqrt(lax.optimization_barrier(jnp.sum(inputs * inputs, axis=1)) / D + 1e-05)
    normed = (inputs * inv_rms[:, None] * norm_gain[None, :]).astype(jnp.bfloat16)
    gate_val = blocked([(normed, gate_weight)], N_ROW)
    up_val = blocked([(normed, up_weight)], N_ROW)
    activated, sigma = silu_parts(gate_val)
    hidden = (activated * up_val).astype(jnp.bfloat16)
    residual = (inputs + blocked([(hidden, down_weight)], col_parts)).astype(jnp.bfloat16)
    predicted = blocked([(residual, proj_weight)], N_ROW)
    keep = loss_mask.astype(jnp.float32)
    error = predicted - teacher_out.astype(jnp.float32)
    masked = error * keep[:, None]
    loss_value = 0.5 * jnp.sum(masked * error) / jnp.sum(keep)
    pred_grad = masked.astype(jnp.bfloat16)
    grad_proj = contract_rows(residual, pred_grad)
    resid_grad = blocked([(pred_grad, proj_weight.T)], col_parts).astype(jnp.bfloat16)
    grad_down = contract_rows(hidden, resid_grad)
    hid_grad = blocked([(resid_grad, down_weight.T)], N_ROW)
    slope = sigma * (1.0 + gate_val * (1.0 - sigma))
    gate_grad = (hid_grad * up_val * slope).astype(jnp.bfloat16)
    up_grad = (hid_grad * activated).astype(jnp.bfloat16)
    grad_gate = contract_rows(normed, gate_grad)
    grad_up = contract_rows(normed, up_grad)
    normed_grad = blocked([(gate_grad, gate_weight.T), (up_grad, up_weight.T)], col_parts)
    grad_gain = lax.optimization_barrier(jnp.sum(normed_grad * inputs * inv_rms[:, None], axis=0))
    inner = lax.optimization_barrier(jnp.sum(normed_grad * norm_gain[None, :] * inputs, axis=1))
    grad_input = resid_grad.astype(jnp.float32) + inv_rms[:, None] * (norm_gain[None, :] * normed_grad) - inputs * (inv_rms * inv_rms * inv_rms * inner / D)[:, None]
    return (loss_value, grad_gain, grad_gate, grad_up, grad_down, grad_proj, grad_input)
```

```python
import jax
import jax.numpy as jnp
from jax import lax
from jax.sharding import PartitionSpec as P

PLANE = ("col", "section")
F32 = jnp.float32
BF16 = jnp.bfloat16


def mm(left, right):
    return jnp.dot(left, right, preferred_element_type=F32)


def mm_t(left, right):
    return lax.dot_general(left, right, (((1,), (1,)), ((), ())), preferred_element_type=F32)


def t_mm(left, right):
    return lax.dot_general(left, right, (((0,), (0,)), ((), ())), preferred_element_type=F32)


def reverse_bits(value, width):
    out = 0
    for bit in range(width):
        out |= ((value >> bit) & 1) << (width - 1 - bit)
    return out


class Plane:
    def __init__(self, size):
        self.size = size
        self.width = (size // 2).bit_length() - 1
        assert 2 << self.width == size
        self.rev = [reverse_bits(k, self.width) for k in range(size // 2)]
        self.perms = []
        for step in range(self.width):
            even, odd = 2 << step, 2 << (self.width - 1 - step)
            self.perms.append([(c, c ^ (odd if c & 1 else even)) for c in range(size)])
        self.swap = [(c, c ^ 1) for c in range(size)]

    def gather(self, block):
        own = block
        for perm in self.perms:
            own = jnp.concatenate([own, lax.ppermute(own, PLANE, perm)], axis=0)
        other = lax.ppermute(own, PLANE, self.swap)
        b = block.shape[0]
        parts = []
        for k in range(self.size // 2):
            j = self.rev[k]
            parts += [own[k * b : (k + 1) * b], other[j * b : (j + 1) * b]]
        return jnp.concatenate(parts, axis=0)

    def scatter(self, full):
        b = full.shape[0] // self.size
        block = lambda i: full[i * b : (i + 1) * b]
        half = self.size // 2
        mine = jnp.concatenate([block(2 * k) for k in range(half)], axis=0)
        send = jnp.concatenate([block(2 * self.rev[k] + 1) for k in range(half)], axis=0)
        got = lax.ppermute(send, PLANE, self.swap)
        acc = mine.astype(F32) + got.astype(F32)
        for perm in reversed(self.perms):
            half = acc.shape[0] // 2
            got = lax.ppermute(acc[half:].astype(BF16), PLANE, perm)
            acc = acc[:half] + got.astype(F32)
        return acc

    def total(self, value):
        for perm in self.perms + [self.swap]:
            value = value + lax.ppermute(value, PLANE, perm)
        return value


class Rows:
    def __init__(self, size, plane):
        self.size = size
        self.ring = [(r, (r + 1) % size) for r in range(size)]
        self.plane = plane
        self.me = lax.axis_index("row")
        c = lax.axis_index(PLANE)
        self.odd = (c & 1) == 1
        self.chip = c >> 1

    def owner(self, back):
        return lax.rem(self.me + (self.size - back), self.size)

    def start(self, owner, rows):
        k = self.chip ^ owner
        flipped = jnp.asarray(self.plane.rev, jnp.int32)[k]
        return jnp.where(self.odd, flipped, k) * rows

    def part(self, full, owner):
        rows = full.shape[0] // self.size
        return lax.dynamic_slice_in_dim(full, self.start(owner, rows), rows, 0)

    def place(self, full, block, owner):
        rows = block.shape[0]
        return lax.dynamic_update_slice_in_dim(full, block, self.start(owner, rows), 0)

    def shift(self, value):
        return lax.ppermute(value, "row", self.ring)

    def reduce(self, left, weights):
        got = None
        for back in range(1, self.size + 1):
            rows = self.part(left, self.owner(back))
            sums = [mm(rows, w) if not t else mm_t(rows, w) for w, t in weights]
            if got is not None:
                sums = [s + g.astype(F32) for s, g in zip(sums, got)]
            if back < self.size:
                got = [self.shift(s.astype(BF16)) for s in sums]
        return sums

    def gather(self, blocks, product):
        fulls, out = None, None
        for back in range(self.size):
            owner = self.owner(back)
            sent = [self.shift(b) for b in blocks] if back < self.size - 1 else None
            made = product(blocks)
            if fulls is None:
                fulls = [jnp.zeros((b.shape[0] * self.size,) + b.shape[1:], b.dtype) for b in blocks]
                out = jnp.zeros((made.shape[0] * self.size,) + made.shape[1:], made.dtype)
            fulls = [self.place(f, b, owner) for f, b in zip(fulls, blocks)]
            out = self.place(out, made, owner)
            blocks = sent
        return fulls, out

    def total(self, value):
        step = 1
        while step < self.size:
            value = value + lax.ppermute(value, "row", [(r, r ^ step) for r in range(self.size)])
            step *= 2
        return value

    def own_order(self, value):
        half = value.shape[0] // 2
        return jnp.where(self.odd, jnp.concatenate([value[half:], value[:half]], axis=0), value)


def make_body(n_row, n_plane):
    plane = Plane(n_plane)
    assert n_plane == 2 * n_row

    def body(x, gain, gate_w, up_w, down_w, proj_w, teacher, loss_mask):
        rows = Rows(n_row, plane)
        block = x.shape[0]
        features = x.shape[1] * n_row

        x_all = plane.gather(x)
        scaled = (x_all.astype(F32) * gain[None, :]).astype(BF16)
        squares = rows.total(jnp.sum(jnp.square(x_all.astype(F32)), axis=1))
        inv_all = lax.rsqrt(squares / features + 1e-05)
        inv = rows.part(inv_all, rows.me)[:, None]

        target = rows.own_order(
            lax.all_to_all(teacher, PLANE, split_axis=1, concat_axis=0, tiled=True)
        ).astype(F32)
        keep = rows.own_order(loss_mask.astype(F32))

        gate, up = rows.reduce(scaled, [(gate_w, False), (up_w, False)])
        gate, up = gate * inv, up * inv
        sigma = jax.nn.sigmoid(gate)
        activated = gate * sigma
        hidden = (activated * up).astype(BF16)
        (hidden_all,), ffn = rows.gather([hidden], lambda b: mm(b[0], down_w).astype(BF16))
        residual = (x.astype(F32) + plane.scatter(ffn)).astype(BF16)
        residual_all = plane.gather(residual)

        (predicted,) = rows.reduce(residual_all, [(proj_w, False)])
        error = predicted - target
        masked = error * keep[:, None]
        loss_parts = jnp.stack([0.5 * jnp.sum(masked * error), jnp.sum(keep)])
        loss_parts = rows.total(plane.total(loss_parts))
        loss_value = loss_parts[0] / (loss_parts[1] / n_plane)

        (pred_grad_all,), back = rows.gather(
            [masked.astype(BF16)], lambda b: mm_t(b[0], proj_w).astype(BF16)
        )
        grad_proj = t_mm(residual_all, pred_grad_all)
        resid_grad = plane.scatter(back).astype(BF16)
        resid_grad_all = plane.gather(resid_grad)
        grad_down = t_mm(hidden_all, resid_grad_all)

        (hid_grad,) = rows.reduce(resid_grad_all, [(down_w, True)])
        gate_grad = hid_grad * up * (sigma * (1.0 + gate * (1.0 - sigma)))
        up_grad = hid_grad * activated
        inner = rows.own_order(jnp.sum(gate_grad * gate + up_grad * up, axis=1))
        inner = plane.total(inner)
        (gate_grad_all, up_grad_all), back = rows.gather(
            [(gate_grad * inv).astype(BF16), (up_grad * inv).astype(BF16)],
            lambda b: (mm_t(b[0], gate_w) + mm_t(b[1], up_w)).astype(BF16),
        )
        grad_gate = t_mm(scaled, gate_grad_all)
        grad_up = t_mm(scaled, up_grad_all)
        grad_gain = plane.total(jnp.sum(back.astype(F32) * x_all.astype(F32), axis=0))
        normed_grad = plane.scatter(back)

        spread = jnp.zeros((n_row, inner.shape[0]), F32)
        spread = lax.dynamic_update_slice_in_dim(spread, inner[None, :], rows.me, 0)
        inner = lax.dynamic_slice_in_dim(
            rows.total(spread).reshape(-1), lax.axis_index(PLANE) * block, block, 0
        )
        inv_own = inv_all[:block]
        grad_input = (
            resid_grad.astype(F32)
            + gain[None, :] * normed_grad
            - x.astype(F32) * (inv_own * inv_own * inner / features)[:, None]
        )
        return (loss_value, grad_gain, grad_gate, grad_up, grad_down, grad_proj, grad_input)

    return body


def solution(mesh):
    in_specs = (
        P(PLANE, "row"),
        P("row"),
        P("row", PLANE),
        P("row", PLANE),
        P(PLANE, "row"),
        P("row", PLANE),
        P(("row", "col", "section"), None),
        P("row"),
    )
    out_specs = (
        P(),
        P("row"),
        P("row", PLANE),
        P("row", PLANE),
        P(PLANE, "row"),
        P("row", PLANE),
        P(PLANE, "row"),
    )
    body = make_body(mesh.shape["row"], mesh.shape["col"] * mesh.shape["section"])
    return jax.shard_map(body, mesh=mesh, in_specs=in_specs, out_specs=out_specs, check_vma=False)
```

```python
import jax
import jax.numpy as jnp
from jax import lax
from jax.sharding import PartitionSpec as P

PLANE = ("col", "section")
F32 = jnp.float32
BF16 = jnp.bfloat16


def mm(left, right):
    return jnp.dot(left, right, preferred_element_type=F32)


def mm_t(left, right):
    return lax.dot_general(left, right, (((1,), (1,)), ((), ())), preferred_element_type=F32)


def t_mm(left, right):
    return lax.dot_general(left, right, (((0,), (0,)), ((), ())), preferred_element_type=F32)


def reverse_bits(value, width):
    out = 0
    for bit in range(width):
        out |= ((value >> bit) & 1) << (width - 1 - bit)
    return out


def after(value, *earlier):
    return lax.optimization_barrier((value,) + earlier)[0]


def halves(size):
    return [(0, size // 2), (size // 2, size)]


class Plane:
    def __init__(self, size):
        self.size = size
        self.width = (size // 2).bit_length() - 1
        assert 2 << self.width == size
        self.rev = [reverse_bits(k, self.width) for k in range(size // 2)]
        self.perms = []
        for step in range(self.width):
            even, odd = 2 << step, 2 << (self.width - 1 - step)
            self.perms.append([(c, c ^ (odd if c & 1 else even)) for c in range(size)])
        self.swap = [(c, c ^ 1) for c in range(size)]

    def gather(self, block):
        own = block
        for perm in self.perms:
            own = jnp.concatenate([own, lax.ppermute(own, PLANE, perm)], axis=0)
        other = lax.ppermute(own, PLANE, self.swap)
        b = block.shape[0]
        parts = []
        for k in range(self.size // 2):
            j = self.rev[k]
            parts += [own[k * b : (k + 1) * b], other[j * b : (j + 1) * b]]
        return jnp.concatenate(parts, axis=0)

    def scatter(self, full):
        b = full.shape[0] // self.size
        block = lambda i: full[i * b : (i + 1) * b]
        half = self.size // 2
        mine = jnp.concatenate([block(2 * k) for k in range(half)], axis=0)
        send = jnp.concatenate([block(2 * self.rev[k] + 1) for k in range(half)], axis=0)
        got = lax.ppermute(send, PLANE, self.swap)
        acc = mine.astype(F32) + got.astype(F32)
        for perm in reversed(self.perms):
            half = acc.shape[0] // 2
            got = lax.ppermute(acc[half:].astype(BF16), PLANE, perm)
            acc = acc[:half] + got.astype(F32)
        return acc

    def total(self, value):
        for perm in self.perms + [self.swap]:
            value = value + lax.ppermute(value, PLANE, perm)
        return value


class Rows:
    def __init__(self, size, plane):
        self.size = size
        self.ring = [(r, (r + 1) % size) for r in range(size)]
        self.plane = plane
        self.me = lax.axis_index("row")
        c = lax.axis_index(PLANE)
        self.odd = (c & 1) == 1
        self.chip = c >> 1

    def owner(self, back):
        return lax.rem(self.me + (self.size - back), self.size)

    def start(self, owner, rows):
        k = self.chip ^ owner
        flipped = jnp.asarray(self.plane.rev, jnp.int32)[k]
        return jnp.where(self.odd, flipped, k) * rows

    def part(self, full, owner):
        rows = full.shape[0] // self.size
        return lax.dynamic_slice_in_dim(full, self.start(owner, rows), rows, 0)

    def place(self, full, block, owner):
        rows = block.shape[0]
        return lax.dynamic_update_slice_in_dim(full, block, self.start(owner, rows), 0)

    def shift(self, value):
        return lax.ppermute(value, "row", self.ring)

    def reduce(self, left, products):
        got = None
        for back in range(1, self.size + 1):
            rows = self.part(left, self.owner(back))
            sums = [product(rows) for product in products]
            if got is not None:
                sums = [s + g.astype(F32) for s, g in zip(sums, got)]
            if back < self.size:
                got = [self.shift(s.astype(BF16)) for s in sums]
        return sums

    def gather(self, blocks, product, first=None):
        fulls, out = None, None
        for back in range(self.size):
            owner = self.owner(back)
            sent = [self.shift(b) for b in blocks] if back < self.size - 1 else None
            if back == 1 and first is not None:
                first.extend(blocks)
            made = product(blocks)
            if fulls is None:
                fulls = [jnp.zeros((b.shape[0] * self.size,) + b.shape[1:], b.dtype) for b in blocks]
                out = jnp.zeros((made.shape[0] * self.size,) + made.shape[1:], made.dtype)
            fulls = [self.place(f, b, owner) for f, b in zip(fulls, blocks)]
            out = self.place(out, made, owner)
            blocks = sent
        return fulls, out

    def total(self, value):
        step = 1
        while step < self.size:
            value = value + lax.ppermute(value, "row", [(r, r ^ step) for r in range(self.size)])
            step *= 2
        return value

    def own_order(self, value):
        half = value.shape[0] // 2
        return jnp.where(self.odd, jnp.concatenate([value[half:], value[:half]], axis=0), value)


def make_body(n_row, n_plane):
    plane = Plane(n_plane)
    assert n_plane == 2 * n_row

    def body(x, gain, gate_w, up_w, down_w, proj_w, teacher, loss_mask):
        rows = Rows(n_row, plane)
        block = x.shape[0]
        features = x.shape[1] * n_row

        x_all = plane.gather(x)
        scaled = (x_all.astype(F32) * gain[None, :]).astype(BF16)
        squares = rows.total(jnp.sum(jnp.square(x_all.astype(F32)), axis=1))
        inv_all = lax.rsqrt(squares / features + 1e-05)
        inv = rows.part(inv_all, rows.me)[:, None]

        target = lax.all_to_all(
            after(teacher, x_all), PLANE, split_axis=1, concat_axis=0, tiled=True
        )
        target = rows.own_order(target).astype(F32)
        keep = rows.own_order(loss_mask.astype(F32))

        gate, up = rows.reduce(scaled, [lambda a: mm(a, gate_w), lambda a: mm(a, up_w)])
        gate, up = gate * inv, up * inv
        sigma = jax.nn.sigmoid(gate)
        activated = gate * sigma
        hidden = after((activated * up).astype(BF16), target)
        cuts = halves(hidden.shape[1])
        hidden_all, ffn = rows.gather(
            [hidden[:, lo:hi] for lo, hi in cuts],
            lambda bs: sum(mm(b, down_w[lo:hi]) for b, (lo, hi) in zip(bs, cuts)).astype(BF16),
        )
        residual = (x.astype(F32) + plane.scatter(ffn)).astype(BF16)
        residual_all = plane.gather(residual)

        ecuts = halves(proj_w.shape[1])
        predicted = rows.reduce(
            residual_all, [lambda a, lo=lo, hi=hi: mm(a, proj_w[:, lo:hi]) for lo, hi in ecuts]
        )
        error = [p - target[:, lo:hi] for p, (lo, hi) in zip(predicted, ecuts)]
        masked = [e * keep[:, None] for e in error]

        moved = []
        pred_grad_all, back = rows.gather(
            [m.astype(BF16) for m in masked],
            lambda bs: sum(mm_t(b, proj_w[:, lo:hi]) for b, (lo, hi) in zip(bs, ecuts)).astype(BF16),
            moved,
        )
        resid_grad = plane.scatter(back).astype(BF16)
        resid_grad_all = plane.gather(resid_grad)

        hid_grad = jnp.concatenate(
            rows.reduce(
                resid_grad_all, [lambda a, lo=lo, hi=hi: mm_t(a, down_w[lo:hi]) for lo, hi in cuts]
            ),
            axis=1,
        )
        gate_grad = hid_grad * up * (sigma * (1.0 + gate * (1.0 - sigma)))
        up_grad = hid_grad * activated
        moved = []
        (gate_grad_all, up_grad_all), back = rows.gather(
            [(gate_grad * inv).astype(BF16), (up_grad * inv).astype(BF16)],
            lambda b: (mm_t(b[0], gate_w) + mm_t(b[1], up_w)).astype(BF16),
            moved,
        )
        normed_grad = plane.scatter(back)
        grad_gain = plane.total(jnp.sum(back.astype(F32) * x_all.astype(F32), axis=0))

        inner = rows.own_order(jnp.sum(gate_grad * gate + up_grad * up, axis=1))
        loss_parts = jnp.stack([0.5 * sum(jnp.sum(m * e) for m, e in zip(masked, error)), jnp.sum(keep)])
        inner = plane.total(after(jnp.concatenate([inner, loss_parts]), *moved))
        loss_parts = rows.total(inner[-2:])
        loss_value = loss_parts[0] / (loss_parts[1] / n_plane)
        spread = jnp.zeros((n_row, inner.shape[0] - 2), F32)
        spread = lax.dynamic_update_slice_in_dim(spread, inner[None, :-2], rows.me, 0)
        inner = lax.dynamic_slice_in_dim(
            rows.total(spread).reshape(-1), lax.axis_index(PLANE) * block, block, 0
        )
        grad_proj = t_mm(after(residual_all, *moved), jnp.concatenate(pred_grad_all, axis=1))
        grad_down = t_mm(after(jnp.concatenate(hidden_all, axis=1), *moved), resid_grad_all)
        grad_gate = t_mm(scaled, gate_grad_all)
        grad_up = t_mm(scaled, up_grad_all)

        inv_own = inv_all[:block]
        grad_input = (
            resid_grad.astype(F32)
            + gain[None, :] * normed_grad
            - x.astype(F32) * (inv_own * inv_own * inner / features)[:, None]
        )
        return (loss_value, grad_gain, grad_gate, grad_up, grad_down, grad_proj, grad_input)

    return body


def solution(mesh):
    in_specs = (
        P(PLANE, "row"),
        P("row"),
        P("row", PLANE),
        P("row", PLANE),
        P(PLANE, "row"),
        P("row", PLANE),
        P(("row", "col", "section"), None),
        P("row"),
    )
    out_specs = (
        P(),
        P("row"),
        P("row", PLANE),
        P("row", PLANE),
        P(PLANE, "row"),
        P("row", PLANE),
        P(PLANE, "row"),
    )
    body = make_body(mesh.shape["row"], mesh.shape["col"] * mesh.shape["section"])
    return jax.shard_map(body, mesh=mesh, in_specs=in_specs, out_specs=out_specs, check_vma=False)
```

```python
import functools

import jax
import jax.numpy as jnp
from jax import lax
from jax.experimental import pallas as pl
from jax.experimental.pallas import tpu as pltpu
from jax.sharding import PartitionSpec as P

PLANE = ("col", "section")
ALL = ("row", "col", "section")
F32 = jnp.float32
BF16 = jnp.bfloat16


def mm(left, right):
    return jnp.dot(left, right, preferred_element_type=F32)


def mm_t(left, right):
    return lax.dot_general(left, right, (((1,), (1,)), ((), ())), preferred_element_type=F32)


def after(value, *earlier):
    return lax.optimization_barrier((value,) + earlier)[0]


def grad_kernel(count, tile, *refs):
    lefts, rights = refs[:count], refs[count : 2 * count]
    out_ref, left, right, sems = refs[2 * count :]
    rows = lefts[0].shape[0]

    @pl.when(pl.program_id(0) == 0)
    def load():
        copies = []
        for i in range(count):
            span = pl.ds(i * rows, rows)
            copies.append(pltpu.make_async_copy(lefts[i], left.at[span], sems.at[2 * i]))
            copies.append(pltpu.make_async_copy(rights[i], right.at[span], sems.at[2 * i + 1]))
        for copy in copies:
            copy.start()
        for copy in copies:
            copy.wait()

    columns = pl.ds(pl.multiple_of(pl.program_id(0) * tile, tile), tile)
    out_ref[...] = lax.dot_general(
        left[:, columns], right[...], (((0,), (0,)), ((), ())), preferred_element_type=F32
    )


def weight_grad(lefts, rights):
    count, rows = len(lefts), lefts[0].shape[0]
    m, n = lefts[0].shape[1], rights[0].shape[1]
    tile = 256 if m % 256 == 0 else 128
    depth = count * rows
    return pl.pallas_call(
        functools.partial(grad_kernel, count, tile),
        grid=(m // tile,),
        in_specs=[pl.BlockSpec(memory_space=pl.ANY)] * (2 * count),
        out_specs=pl.BlockSpec((tile, n), lambda i: (i, 0)),
        out_shape=jax.ShapeDtypeStruct((m, n), F32),
        scratch_shapes=[
            pltpu.VMEM((depth, m), BF16),
            pltpu.VMEM((depth, n), BF16),
            pltpu.SemaphoreType.DMA((2 * count,)),
        ],
        compiler_params=pltpu.CompilerParams(vmem_limit_bytes=24 << 20),
        cost_estimate=pl.CostEstimate(
            flops=2 * depth * m * n,
            bytes_accessed=2 * depth * (m + n) + 4 * m * n,
            transcendentals=0,
        ),
    )(*lefts, *rights)


class Moves:
    def __init__(self, n_row, n_plane):
        assert n_plane == 2 * n_row
        self.n_row, self.n_plane = n_row, n_plane
        self.ring = [(r, (r + 1) % n_row) for r in range(n_row)]
        self.swap = [(c, c ^ 1) for c in range(n_plane)]
        self.meet = []
        for back in range(n_row):
            pairs = []
            for r in range(n_row):
                for c in range(n_plane):
                    pairs.append((r * n_plane + c, r * n_plane + (c ^ (2 * ((r - back) % n_row)))))
            self.meet.append(pairs)

    def to_core(self, value):
        return lax.ppermute(value, PLANE, self.swap)

    def to_chip(self, value, back):
        return lax.ppermute(value, ALL, self.meet[back])

    def to_next(self, value):
        return lax.ppermute(value, "row", self.ring)

    def plane_gather(self, block):
        order = list(range(1, self.n_row)) + [0]
        own = {back: self.to_chip(block, back) for back in order}
        other = {back: self.to_core(own[back]) for back in order}
        return [[own[b] for b in range(self.n_row)], [other[b] for b in range(self.n_row)]]

    def plane_scatter(self, made):
        total = 0.0
        for back in range(self.n_row):
            both = made[0][back].astype(F32) + self.to_core(made[1][back]).astype(F32)
            total = total + self.to_chip(both.astype(BF16), back).astype(F32)
        return total

    def row_reduce(self, pieces, products):
        got = [None, None]
        for back in range(1, self.n_row + 1):
            for s in range(2):
                sums = [product(pieces[s][back % self.n_row]) for product in products]
                if got[s] is not None:
                    sums = [a + b.astype(F32) for a, b in zip(sums, got[s])]
                if back < self.n_row:
                    sums = [self.to_next(a.astype(BF16)) for a in sums]
                got[s] = sums
        return got

    def row_gather(self, blocks, product):
        pieces = [[list(blocks[s])] for s in range(2)]
        for back in range(1, self.n_row):
            for s in range(2):
                pieces[s].append([self.to_next(a) for a in pieces[s][-1]])
        made = [[product(piece) for piece in pieces[s]] for s in range(2)]
        return pieces, made

    def total(self, value, axes, size):
        step = 1
        while step < size:
            value = value + lax.ppermute(value, axes, [(i, i ^ step) for i in range(size)])
            step *= 2
        return value

    def row_total(self, value):
        return self.total(value, "row", self.n_row)

    def plane_total(self, value):
        return self.total(value, PLANE, self.n_plane)


def make_body(n_row, n_plane):
    moves = Moves(n_row, n_plane)

    def body(x, gain, gate_w, up_w, down_w, proj_w, teacher, loss_mask):
        block = x.shape[0]
        features = x.shape[1] * n_row
        c = lax.axis_index(PLANE)
        odd = (c & 1) == 1
        chip = (c >> 1) ^ lax.axis_index("row")

        def streams(value):
            low, high = value[:block], value[block:]
            return [jnp.where(odd, high, low), jnp.where(odd, low, high)]

        def every(pieces, at=None):
            return [p if at is None else p[at] for stream in pieces for p in stream]

        by_chip = teacher.reshape(teacher.shape[0], n_row, -1)
        by_chip = [by_chip[:, :1]] + [
            lax.ppermute(by_chip[:, p : p + 1], "row", [(r, r ^ p) for r in range(n_row)])
            for p in range(1, n_row)
        ]
        mine = [
            (r * n_plane + i, ((i >> 1) ^ r) * n_plane + i)
            for r in range(n_row)
            for i in range(n_plane)
        ]
        keep = streams(lax.ppermute(loss_mask, ALL, mine).astype(F32))

        x_pieces = moves.plane_gather(x)
        scaled = [
            [(p.astype(F32) * gain[None, :]).astype(BF16) for p in stream] for stream in x_pieces
        ]
        scaled[0][1] = after(scaled[0][1], *by_chip)
        by_chip = jnp.concatenate(by_chip, axis=1).reshape(teacher.shape)
        target = lax.all_to_all(by_chip, PLANE, split_axis=1, concat_axis=0, tiled=True)
        target = streams(target)

        squares = moves.row_total(jnp.sum(jnp.square(x.astype(F32)), axis=1))
        inv_own = lax.rsqrt(squares / features + 1e-05)
        inv = [moves.to_chip(inv_own, 0)]
        inv.append(moves.to_core(inv[0]))
        inv = [i[:, None] for i in inv]

        sums = moves.row_reduce(scaled, [lambda a: mm(a, gate_w), lambda a: mm(a, up_w)])
        gate = [sums[s][0] * inv[s] for s in range(2)]
        up = [sums[s][1] * inv[s] for s in range(2)]
        sigma = [jax.nn.sigmoid(g) for g in gate]
        activated = [g * z for g, z in zip(gate, sigma)]
        hidden = [[after((activated[s] * up[s]).astype(BF16), target[s])] for s in range(2)]
        hidden, ffn = moves.row_gather(hidden, lambda a: mm(a[0], down_w).astype(BF16))
        residual = (x.astype(F32) + moves.plane_scatter(ffn)).astype(BF16)
        residual = moves.plane_gather(residual)

        sums = moves.row_reduce(residual, [lambda a: mm(a, proj_w)])
        error = [sums[s][0] - target[s].astype(F32) for s in range(2)]
        masked = [error[s] * keep[s][:, None] for s in range(2)]
        pred_grad, back = moves.row_gather(
            [[m.astype(BF16)] for m in masked], lambda a: mm_t(a[0], proj_w).astype(BF16)
        )
        resid_grad = moves.plane_scatter(back).astype(BF16)
        resid_grads = moves.plane_gather(resid_grad)

        sums = moves.row_reduce(resid_grads, [lambda a: mm_t(a, down_w)])
        hid_grad = [sums[s][0] for s in range(2)]
        gate_grad = [
            hid_grad[s] * up[s] * (sigma[s] * (1.0 + gate[s] * (1.0 - sigma[s]))) for s in range(2)
        ]
        up_grad = [hid_grad[s] * activated[s] for s in range(2)]
        grads, back = moves.row_gather(
            [[(gate_grad[s] * inv[s]).astype(BF16), (up_grad[s] * inv[s]).astype(BF16)] for s in range(2)],
            lambda a: (mm_t(a[0], gate_w) + mm_t(a[1], up_w)).astype(BF16),
        )
        normed_grad = moves.plane_scatter(back)
        grad_gain = moves.plane_total(
            sum(
                jnp.sum(b.astype(F32) * a.astype(F32), axis=0)
                for b, a in zip(every(back), every(x_pieces))
            )
        )

        moved = grads[0][1]
        inner = [jnp.sum(gate_grad[s] * gate[s] + up_grad[s] * up[s], axis=1) for s in range(2)]
        inner = jnp.concatenate(streams(jnp.concatenate(inner)))
        parts = jnp.zeros((n_row, 2 * block), F32)
        parts = lax.dynamic_update_slice_in_dim(parts, inner[None, :], chip, 0).reshape(-1)
        loss_sum = sum(0.5 * jnp.sum(m * e) for m, e in zip(masked, error))
        loss_parts = jnp.stack([loss_sum, sum(jnp.sum(k) for k in keep)])
        parts = after(jnp.concatenate([parts, loss_parts]), *moved)
        parts = moves.row_total(moves.plane_total(parts))
        loss_value = parts[-2] / (parts[-1] / n_plane)
        inner = lax.dynamic_slice_in_dim(parts, c * block, block, 0)

        grad_proj = weight_grad(every(residual), every(pred_grad, 0))
        hiddens = every(hidden, 0)
        hiddens[0] = after(hiddens[0], *moved)
        grad_down = weight_grad(hiddens, every(resid_grads))
        grad_gate = weight_grad(every(scaled), every(grads, 0))
        grad_up = weight_grad(every(scaled), every(grads, 1))

        grad_input = (
            resid_grad.astype(F32)
            + gain[None, :] * normed_grad
            - x.astype(F32) * (inv_own * inv_own * inner / features)[:, None]
        )
        return (loss_value, grad_gain, grad_gate, grad_up, grad_down, grad_proj, grad_input)

    return body


def solution(mesh):
    in_specs = (
        P(PLANE, "row"),
        P("row"),
        P("row", PLANE),
        P("row", PLANE),
        P(PLANE, "row"),
        P("row", PLANE),
        P(ALL, None),
        P("row"),
    )
    out_specs = (
        P(),
        P("row"),
        P("row", PLANE),
        P("row", PLANE),
        P(PLANE, "row"),
        P("row", PLANE),
        P(PLANE, "row"),
    )
    body = make_body(mesh.shape["row"], mesh.shape["col"] * mesh.shape["section"])
    return jax.shard_map(body, mesh=mesh, in_specs=in_specs, out_specs=out_specs, check_vma=False)
```

```python
import functools

import jax
import jax.numpy as jnp
from jax import lax
from jax.experimental import pallas as pl
from jax.experimental.pallas import tpu as pltpu
from jax.sharding import PartitionSpec as P

PLANE = ("col", "section")
ALL = ("row", "col", "section")
F32 = jnp.float32
BF16 = jnp.bfloat16
HALVES = 2


def mm(left, right):
    return jnp.dot(left, right, preferred_element_type=F32)


def mm_t(left, right):
    return lax.dot_general(left, right, (((1,), (1,)), ((), ())), preferred_element_type=F32)


def t_mm(left, right):
    return lax.dot_general(left, right, (((0,), (0,)), ((), ())), preferred_element_type=F32)


def after(value, earlier):
    first = earlier[(0,) * earlier.ndim]
    return jnp.where(first == first, value, jnp.zeros_like(value))


def assemble_kernel(plan, rows, starts, *refs):
    pieces, out, sems = refs[:-2], refs[-2], refs[-1]
    copies = []
    for i, (piece, at) in enumerate(plan):
        to = pl.multiple_of(starts[i] * rows, rows)
        copies.append(
            pltpu.make_async_copy(pieces[piece].at[pl.ds(at, rows)], out.at[pl.ds(to, rows)], sems.at[i])
        )
    for copy in copies:
        copy.start()
    for copy in copies:
        copy.wait()


def assemble(pieces, plan, starts, rows):
    width = pieces[0].shape[1]
    return pl.pallas_call(
        functools.partial(assemble_kernel, plan, rows),
        in_specs=[pl.BlockSpec(memory_space=pltpu.SMEM)]
        + [pl.BlockSpec(memory_space=pl.ANY)] * len(pieces),
        out_specs=pl.BlockSpec(memory_space=pl.ANY),
        out_shape=jax.ShapeDtypeStruct((len(plan) * rows, width), pieces[0].dtype),
        scratch_shapes=[pltpu.SemaphoreType.DMA((len(plan),))],
        cost_estimate=pl.CostEstimate(
            flops=0, bytes_accessed=4 * len(plan) * rows * width, transcendentals=0
        ),
    )(starts, *pieces)


def reverse_bits(value, width):
    out = 0
    for bit in range(width):
        out |= ((value >> bit) & 1) << (width - 1 - bit)
    return out


class Moves:
    def __init__(self, n_row, n_plane):
        assert n_plane == 2 * n_row
        self.n_row, self.n_plane = n_row, n_plane
        width = n_row.bit_length() - 1
        assert 1 << width == n_row
        self.rev = [reverse_bits(k, width) for k in range(n_row)]
        self.perms = []
        for step in range(width):
            even, odd = 2 << step, 2 << (width - 1 - step)
            self.perms.append([(c, c ^ (odd if c & 1 else even)) for c in range(n_plane)])
        self.swap = [(c, c ^ 1) for c in range(n_plane)]
        self.ring = [(r, (r + 1) % n_row) for r in range(n_row)]

    def locate(self):
        c, me = lax.axis_index(PLANE), lax.axis_index("row")
        self.odd = (c & 1) == 1
        self.slots = []
        for back in range(self.n_row):
            k = (c >> 1) ^ lax.rem(me + (self.n_row - back), self.n_row)
            flipped = jnp.asarray(self.rev, jnp.int32)[k]
            self.slots.append(jnp.where(self.odd, flipped, k))

    def exchange(self, values, axes, perm, free, arrived, label):
        earlier = yield free
        if earlier is not None:
            values = [after(v, earlier) for v in values]
        with jax.named_scope(label):
            got = [lax.ppermute(v, axes, perm) for v in values]
        arrived.append(got[-1])
        return got

    def plane_gather(self, block, arrived, label):
        own = block
        for perm in self.perms:
            (got,) = yield from self.exchange([own], PLANE, perm, True, arrived, label)
            own = jnp.concatenate([own, got], axis=0)
        (other,) = yield from self.exchange([own], PLANE, self.swap, True, arrived, label)
        rows = block.shape[0]
        plan, starts = [], []
        for k in range(self.n_row):
            plan += [(0, k * rows), (1, self.rev[k] * rows)]
            starts += [2 * k, 2 * k + 1]
        return assemble([own, other], plan, jnp.asarray(starts, jnp.int32), rows)

    def plane_scatter(self, full, arrived, label):
        block = full.shape[0] // self.n_plane
        rows = lambda i: full[i * block : (i + 1) * block]
        mine = jnp.concatenate([rows(2 * k) for k in range(self.n_row)], axis=0)
        send = jnp.concatenate([rows(2 * self.rev[k] + 1) for k in range(self.n_row)], axis=0)
        (got,) = yield from self.exchange([send], PLANE, self.swap, True, arrived, label)
        acc = mine.astype(F32) + got.astype(F32)
        for perm in reversed(self.perms):
            half = acc.shape[0] // 2
            (got,) = yield from self.exchange([acc[half:].astype(BF16)], PLANE, perm, True, arrived, label)
            acc = acc[:half] + got.astype(F32)
        return acc

    def part(self, full, back):
        rows = full.shape[0] // self.n_row
        return lax.dynamic_slice_in_dim(full, self.slots[back] * rows, rows, 0)

    def row_reduce(self, fulls, arrived, label):
        got = None
        for back in range(1, self.n_row + 1):
            sums = [self.part(full, back % self.n_row).astype(F32) for full in fulls]
            if got is not None:
                sums = [a + b.astype(F32) for a, b in zip(sums, got)]
            if back < self.n_row:
                sums = [a.astype(BF16) for a in sums]
                got = yield from self.exchange(sums, "row", self.ring, True, arrived, label)
        return sums

    def row_gather(self, blocks, arrived, label):
        steps = [blocks]
        for back in range(1, self.n_row):
            got = yield from self.exchange(steps[-1], "row", self.ring, back == 1, arrived, label)
            steps.append(got)
        plan = [(back, 0) for back in range(self.n_row)]
        starts = jnp.stack(self.slots)
        rows = blocks[0].shape[0]
        return [assemble(list(p), plan, starts, rows) for p in zip(*steps)]

    def total(self, value, axes, size):
        step = 1
        while step < size:
            value = value + lax.ppermute(value, axes, [(i, i ^ step) for i in range(size)])
            step *= 2
        return value

    def row_total(self, value):
        return self.total(value, "row", self.n_row)

    def plane_total(self, value):
        return self.total(value, PLANE, self.n_plane)


def alone(steps):
    try:
        next(steps)
        while True:
            steps.send(None)
    except StopIteration as end:
        return end.value


def together(halves, arrived, order):
    free = [next(h) for h in halves]
    held, done = [-1, -1], [None, None]
    for h in order:
        seen = len(arrived[1 - h]) - 2
        earlier = None
        if free[h] and seen > held[h]:
            earlier, held[h] = arrived[1 - h][seen], seen
        try:
            free[h] = halves[h].send(earlier)
        except StopIteration as end:
            done[h] = end.value
    return done


PHASES = (
    ("R", 17, 48),
    ("R", 48, 90),
    ("P", 78, 116),
    ("P", 94, 132),
    ("R", 108, 146),
    ("R", 132, 172),
    ("P", 155, 198),
    ("P", 171, 214),
    ("R", 185, 228),
    ("R", 210, 258),
    ("P", 250, 290),
    (None, 268, 308),
)


def step_order(ring_steps, plane_steps):
    events = []
    for h in range(2):
        for (kind, *start), (_, *end) in zip(PHASES, PHASES[1:]):
            steps = ring_steps if kind == "R" else plane_steps
            for i in range(steps):
                events.append((start[h] + (end[h] - start[h]) * i / steps, h))
    return [h for _, h in sorted(events)]


def make_body(n_row, n_plane):
    moves = Moves(n_row, n_plane)

    def body(x, gain, gate_w, up_w, down_w, proj_w, teacher, loss_mask):
        moves.locate()
        half = x.shape[0] // HALVES
        features = x.shape[1] * n_row
        both = range(HALVES)
        odd = moves.odd

        def owned(value):
            value = value.reshape((2, HALVES, half) + value.shape[1:])
            value = jnp.where(odd, value[::-1], value)
            return [value[:, h].reshape((2 * half,) + value.shape[3:]) for h in both]

        def disowned(values):
            value = jnp.stack([v.reshape(2, half) for v in values], axis=1)
            return jnp.where(odd, value[::-1], value).reshape(-1)

        xs = [x[h * half : (h + 1) * half] for h in both]
        x_all = [alone(moves.plane_gather(xs[0], [], "gather_x_a"))]
        x_all.append(alone(moves.plane_gather(after(xs[1], x_all[0]), [], "gather_x_b")))
        scaled = [(v.astype(F32) * gain[None, :]).astype(BF16) for v in x_all]
        squares = [jnp.sum(jnp.square(v.astype(F32)), axis=1) for v in x_all]
        squares = moves.row_total(jnp.concatenate(squares))
        inv_all = lax.rsqrt(squares / features + 1e-05).reshape(HALVES, -1)
        inv = [moves.part(inv_all[h], 0)[:, None] for h in both]

        target = lax.all_to_all(
            after(teacher, x_all[0]), PLANE, split_axis=1, concat_axis=0, tiled=True
        )
        target = owned(target)
        keep = owned(loss_mask.astype(F32))

        arrived = [[], []]

        def steps(h):
            name = lambda what: what + "_" + "ab"[h]
            log = arrived[h]
            fulls = [mm(scaled[h], gate_w).astype(BF16), mm(scaled[h], up_w).astype(BF16)]
            gate, up = yield from moves.row_reduce(fulls, log, name("reduce_gate_up"))
            gate, up = gate * inv[h], up * inv[h]
            sigma = jax.nn.sigmoid(gate)
            activated = gate * sigma
            own = after((activated * up).astype(BF16), target[h])
            (hidden,) = yield from moves.row_gather([own], log, name("gather_hidden"))
            ffn = yield from moves.plane_scatter(mm(hidden, down_w).astype(BF16), log, name("scatter_ffn"))
            residual = (xs[h].astype(F32) + ffn).astype(BF16)
            residual = yield from moves.plane_gather(residual, log, name("gather_residual"))
            fulls = [mm(residual, proj_w).astype(BF16)]
            (predicted,) = yield from moves.row_reduce(fulls, log, name("reduce_predicted"))
            error = predicted - target[h].astype(F32)
            masked = error * keep[h][:, None]
            (pred_grad,) = yield from moves.row_gather([masked.astype(BF16)], log, name("gather_pred_grad"))
            back = yield from moves.plane_scatter(mm_t(pred_grad, proj_w).astype(BF16), log, name("scatter_resid_grad"))
            resid_grad = back.astype(BF16)
            resid_all = yield from moves.plane_gather(resid_grad, log, name("gather_resid_grad"))
            fulls = [mm_t(resid_all, down_w).astype(BF16)]
            (hid_grad,) = yield from moves.row_reduce(fulls, log, name("reduce_hid_grad"))
            gate_grad = hid_grad * up * (sigma * (1.0 + gate * (1.0 - sigma)))
            up_grad = hid_grad * activated
            inner = jnp.sum(gate_grad * gate + up_grad * up, axis=1)
            first = len(log)
            blocks = [(gate_grad * inv[h]).astype(BF16), (up_grad * inv[h]).astype(BF16)]
            gate_all, up_all = yield from moves.row_gather(blocks, log, name("gather_gate_up_grad"))
            back = (mm_t(gate_all, gate_w) + mm_t(up_all, up_w)).astype(BF16)
            gain_sum = jnp.sum(back.astype(F32) * x_all[h].astype(F32), axis=0)
            normed_grad = yield from moves.plane_scatter(back, log, name("scatter_normed_grad"))
            return dict(
                hidden=hidden,
                residual=residual,
                pred_grad=pred_grad,
                resid_grad=resid_grad,
                resid_all=resid_all,
                gate_all=gate_all,
                up_all=up_all,
                normed_grad=normed_grad,
                gain_sum=gain_sum,
                inner=inner,
                loss=0.5 * jnp.sum(masked * error),
                moved=log[first],
            )

        order = step_order(n_row - 1, n_row.bit_length())
        done = together([steps(0), steps(1)], arrived, order)
        each = lambda name: [d[name] for d in done]
        grad_gain = moves.plane_total(sum(each("gain_sum")))

        parts = jnp.zeros((n_row, 2 * HALVES * half), F32)
        parts = lax.dynamic_update_slice_in_dim(
            parts, disowned(each("inner"))[None, :], lax.axis_index("row"), 0
        ).reshape(-1)
        loss_parts = jnp.stack([sum(each("loss")), sum(jnp.sum(k) for k in keep)])
        parts = after(jnp.concatenate([parts, loss_parts]), done[1]["moved"])
        parts = moves.row_total(moves.plane_total(parts))
        loss_value = parts[-2] / (parts[-1] / n_plane)
        inner = lax.dynamic_slice_in_dim(
            parts, lax.axis_index(PLANE) * x.shape[0], x.shape[0], 0
        )

        def whole(values, earlier=None):
            if earlier is not None:
                values = [after(values[0], earlier)] + values[1:]
            return jnp.concatenate(values, axis=0)

        moved = each("moved")
        grad_proj = t_mm(whole(each("residual"), moved[0]), whole(each("pred_grad")))
        grad_down = t_mm(whole(each("hidden"), moved[1]), whole(each("resid_all")))
        scaled = whole(scaled)
        grad_gate = t_mm(scaled, whole(each("gate_all")))
        grad_up = t_mm(scaled, whole(each("up_all")))

        inv_own = inv_all[:, :half].reshape(-1)
        grad_input = (
            jnp.concatenate(each("resid_grad"), axis=0).astype(F32)
            + gain[None, :] * jnp.concatenate(each("normed_grad"), axis=0)
            - x.astype(F32) * (inv_own * inv_own * inner / features)[:, None]
        )
        return (loss_value, grad_gain, grad_gate, grad_up, grad_down, grad_proj, grad_input)

    return body


def solution(mesh):
    in_specs = (
        P(PLANE, "row"),
        P("row"),
        P("row", PLANE),
        P("row", PLANE),
        P(PLANE, "row"),
        P("row", PLANE),
        P(ALL, None),
        P("row"),
    )
    out_specs = (
        P(),
        P("row"),
        P("row", PLANE),
        P("row", PLANE),
        P(PLANE, "row"),
        P("row", PLANE),
        P(PLANE, "row"),
    )
    body = make_body(mesh.shape["row"], mesh.shape["col"] * mesh.shape["section"])
    return jax.shard_map(body, mesh=mesh, in_specs=in_specs, out_specs=out_specs, check_vma=False)
```

```python
import functools

import jax
import jax.numpy as jnp
from jax import lax
from jax.experimental import pallas as pl
from jax.experimental.pallas import tpu as pltpu
from jax.sharding import PartitionSpec as P

PLANE = ("col", "section")
F32 = jnp.float32
BF16 = jnp.bfloat16


def mm(left, right):
    return jnp.dot(left, right, preferred_element_type=F32)


def mm_t(left, right):
    return lax.dot_general(left, right, (((1,), (1,)), ((), ())), preferred_element_type=F32)


def grad_kernel(n_left, tile, *refs):
    out_ref, left, right, sems = refs[-4:]
    pieces = refs[:-4]

    @pl.when(pl.program_id(0) == 0)
    def load():
        copies, at = [], [0, 0]
        for i, piece in enumerate(pieces):
            side = 0 if i < n_left else 1
            to = (left, right)[side].at[pl.ds(at[side], piece.shape[0])]
            at[side] += piece.shape[0]
            copies.append(pltpu.make_async_copy(piece, to, sems.at[i]))
        for copy in copies:
            copy.start()
        for copy in copies:
            copy.wait()

    columns = pl.ds(pl.multiple_of(pl.program_id(0) * tile, tile), tile)
    out_ref[...] = lax.dot_general(
        left[:, columns], right[...], (((0,), (0,)), ((), ())), preferred_element_type=F32
    )


def weight_grad(lefts, rights):
    depth = sum(p.shape[0] for p in lefts)
    m, n = lefts[0].shape[1], rights[0].shape[1]
    tile = 256 if m % 256 == 0 else 128
    pieces = list(lefts) + list(rights)
    return pl.pallas_call(
        functools.partial(grad_kernel, len(lefts), tile),
        grid=(m // tile,),
        in_specs=[pl.BlockSpec(memory_space=pl.ANY)] * len(pieces),
        out_specs=pl.BlockSpec((tile, n), lambda i: (i, 0)),
        out_shape=jax.ShapeDtypeStruct((m, n), F32),
        scratch_shapes=[
            pltpu.VMEM((depth, m), BF16),
            pltpu.VMEM((depth, n), BF16),
            pltpu.SemaphoreType.DMA((len(pieces),)),
        ],
        compiler_params=pltpu.CompilerParams(vmem_limit_bytes=20 << 20),
        cost_estimate=pl.CostEstimate(
            flops=2 * depth * m * n,
            bytes_accessed=2 * depth * (m + n) + 4 * m * n,
            transcendentals=0,
        ),
    )(*pieces)


def reverse_bits(value, width):
    out = 0
    for bit in range(width):
        out |= ((value >> bit) & 1) << (width - 1 - bit)
    return out


def after(value, earlier):
    first = earlier[(0,) * earlier.ndim]
    return jnp.where(first == first, value, jnp.zeros_like(value))


def halves(size):
    return [(0, size // 2), (size // 2, size)]


class Plane:
    def __init__(self, size):
        self.size = size
        self.width = (size // 2).bit_length() - 1
        assert 2 << self.width == size
        self.rev = [reverse_bits(k, self.width) for k in range(size // 2)]
        self.perms = []
        for step in range(self.width):
            even, odd = 2 << step, 2 << (self.width - 1 - step)
            self.perms.append([(c, c ^ (odd if c & 1 else even)) for c in range(size)])
        self.swap = [(c, c ^ 1) for c in range(size)]

    def gather(self, block):
        own = block
        for perm in self.perms:
            own = jnp.concatenate([own, lax.ppermute(own, PLANE, perm)], axis=0)
        return own, lax.ppermute(own, PLANE, self.swap)

    def scatter(self, full, early=False):
        b = full.shape[0] // self.size
        block = lambda i: full[i * b : (i + 1) * b]
        half = self.size // 2
        mine = jnp.concatenate([block(2 * k) for k in range(half)], axis=0)
        send = jnp.concatenate([block(2 * self.rev[k] + 1) for k in range(half)], axis=0)
        got = lax.ppermute(send, PLANE, self.swap)
        first = got
        acc = mine.astype(F32) + got.astype(F32)
        for perm in reversed(self.perms):
            half = acc.shape[0] // 2
            got = lax.ppermute(acc[half:].astype(full.dtype), PLANE, perm)
            acc = acc[:half] + got.astype(F32)
        return (acc, first) if early else acc

    def total(self, value):
        for perm in self.perms + [self.swap]:
            value = value + lax.ppermute(value, PLANE, perm)
        return value


class Rows:
    def __init__(self, size, plane):
        self.size = size
        self.ring = [(r, (r + 1) % size) for r in range(size)]
        self.me = lax.axis_index("row")
        c = lax.axis_index(PLANE)
        self.odd = (c & 1) == 1
        self.slots = []
        for back in range(size):
            k = (c >> 1) ^ lax.rem(self.me + (size - back), size)
            flipped = jnp.asarray(plane.rev, jnp.int32)[k]
            self.slots.append((jnp.where(self.odd, flipped, k), jnp.where(self.odd, k, flipped)))

    def parts(self, own, other):
        b = own.shape[0] // self.size
        return [
            [
                lax.dynamic_slice_in_dim(own, at * b, b, 0),
                lax.dynamic_slice_in_dim(other, at_other * b, b, 0),
            ]
            for at, at_other in self.slots
        ]

    def place(self, full, block, back):
        rows = block.shape[0]
        return lax.dynamic_update_slice_in_dim(full, block, self.slots[back][0] * rows, 0)

    def shift(self, value):
        return lax.ppermute(value, "row", self.ring)

    def reduce(self, parts, products):
        got, first = None, None
        for back in range(1, self.size + 1):
            rows = jnp.concatenate(parts[back % self.size], axis=0)
            sums = [product(rows) for product in products]
            if got is not None:
                sums = [s + g.astype(F32) for s, g in zip(sums, got)]
            if back < self.size:
                got = [self.shift(s.astype(BF16)) for s in sums]
                first = got[0] if first is None else first
        return sums, first

    def gather(self, blocks, product):
        steps = [blocks]
        for back in range(1, self.size):
            steps.append([self.shift(b) for b in steps[-1]])
        made = [product(step) for step in steps]
        return steps, made, self.placed(made)

    def placed(self, blocks):
        out = jnp.zeros((blocks[0].shape[0] * self.size,) + blocks[0].shape[1:], blocks[0].dtype)
        for back, block in enumerate(blocks):
            out = self.place(out, block, back)
        return out

    def total(self, value):
        step = 1
        while step < self.size:
            value = value + lax.ppermute(value, "row", [(r, r ^ step) for r in range(self.size)])
            step *= 2
        return value

    def own_order(self, value):
        half = value.shape[0] // 2
        return jnp.where(self.odd, jnp.concatenate([value[half:], value[:half]], axis=0), value)


def make_body(n_row, n_plane):
    plane = Plane(n_plane)
    assert n_plane == 2 * n_row

    def body(x, gain, gate_w, up_w, down_w, proj_w, teacher, loss_mask):
        rows = Rows(n_row, plane)
        block = x.shape[0]
        features = x.shape[1] * n_row

        own, other = plane.gather(x)
        x_parts = rows.parts(own, other)
        scaled = [[(p.astype(F32) * gain[None, :]).astype(BF16) for p in part] for part in x_parts]
        squares = [jnp.sum(jnp.square(p.astype(F32)), axis=1) for p in (own, other)]
        squares = rows.total(jnp.concatenate(squares))
        inv_all = lax.rsqrt(squares / features + 1e-05)
        inv = jnp.concatenate(rows.parts(*jnp.split(inv_all, 2))[0])[:, None]

        (gate, up), moved = rows.reduce(scaled, [lambda a: mm(a, gate_w), lambda a: mm(a, up_w)])
        target = lax.all_to_all(
            after(teacher, moved), PLANE, split_axis=1, concat_axis=0, tiled=True
        )
        target = rows.own_order(target).astype(F32)
        keep = rows.own_order(loss_mask.astype(F32))
        inv = after(inv, target)
        gate, up = gate * inv, up * inv
        sigma = jax.nn.sigmoid(gate)
        activated = gate * sigma
        hidden = (activated * up).astype(BF16)
        cuts = halves(hidden.shape[1])
        hiddens, _, ffn = rows.gather(
            [hidden[:, lo:hi] for lo, hi in cuts],
            lambda bs: sum(mm(b, down_w[lo:hi]) for b, (lo, hi) in zip(bs, cuts)).astype(BF16),
        )
        residual = (x.astype(F32) + plane.scatter(ffn)).astype(BF16)
        residuals = rows.parts(*plane.gather(residual))

        ecuts = halves(proj_w.shape[1])
        predicted, _ = rows.reduce(
            residuals, [lambda a, lo=lo, hi=hi: mm(a, proj_w[:, lo:hi]) for lo, hi in ecuts]
        )
        error = [p - target[:, lo:hi] for p, (lo, hi) in zip(predicted, ecuts)]
        masked = [e * keep[:, None] for e in error]

        pred_grads, _, back = rows.gather(
            [m.astype(BF16) for m in masked],
            lambda bs: sum(mm_t(b, proj_w[:, lo:hi]) for b, (lo, hi) in zip(bs, ecuts)).astype(BF16),
        )
        resid_grad, swapped = plane.scatter(back, True)
        resid_grad = resid_grad.astype(BF16)
        resid_grads = rows.parts(*plane.gather(resid_grad))

        hid_grad, _ = rows.reduce(
            resid_grads, [lambda a, lo=lo, hi=hi: mm_t(a, down_w[lo:hi]) for lo, hi in cuts]
        )
        hid_grad = jnp.concatenate(hid_grad, axis=1)
        gate_grad = hid_grad * up * (sigma * (1.0 + gate * (1.0 - sigma)))
        up_grad = hid_grad * activated
        inner = jnp.sum(gate_grad * gate + up_grad * up, axis=1)
        grads, made, back = rows.gather(
            [(gate_grad * inv).astype(BF16), (up_grad * inv).astype(BF16), inner],
            lambda b: (mm_t(b[0], gate_w) + mm_t(b[1], up_w)).astype(BF16),
        )
        normed_grad = plane.scatter(back)
        loss_sum = 0.5 * sum(jnp.sum(m * e) for m, e in zip(masked, error))
        loss_parts = rows.total(jnp.stack([loss_sum, jnp.sum(keep)]))
        gain_sum = sum(
            jnp.sum(m.astype(F32) * jnp.concatenate(p, axis=0).astype(F32), axis=0)
            for m, p in zip(made, x_parts)
        )
        sums = plane.total(jnp.concatenate([gain_sum, loss_parts]))
        grad_gain = sums[:-2]
        loss_value = sums[-2] / (sums[-1] / n_plane)

        def pieces(parts, earlier=None):
            parts = [p for part in parts for p in part]
            if earlier is not None:
                parts[0] = after(parts[0], earlier)
            return parts

        whole = lambda steps: [jnp.concatenate(step, axis=1) for step in steps]
        grad_proj = weight_grad(pieces(residuals, swapped), whole(pred_grads))
        grad_down = weight_grad(whole(hiddens), pieces(resid_grads, grads[0][1]))
        inner = plane.scatter(after(rows.placed([g[2] for g in grads]), grad_down))
        grad_gate = weight_grad(pieces(scaled), [g[0] for g in grads])
        grad_up = weight_grad(pieces(scaled), [g[1] for g in grads])

        inv_own = inv_all[:block]
        grad_input = (
            resid_grad.astype(F32)
            + gain[None, :] * normed_grad
            - x.astype(F32) * (inv_own * inv_own * inner / features)[:, None]
        )
        return (loss_value, grad_gain, grad_gate, grad_up, grad_down, grad_proj, grad_input)

    return body


def solution(mesh):
    in_specs = (
        P(PLANE, "row"),
        P("row"),
        P("row", PLANE),
        P("row", PLANE),
        P(PLANE, "row"),
        P("row", PLANE),
        P(("row", "col", "section"), None),
        P("row"),
    )
    out_specs = (
        P(),
        P("row"),
        P("row", PLANE),
        P("row", PLANE),
        P(PLANE, "row"),
        P("row", PLANE),
        P(PLANE, "row"),
    )
    body = make_body(mesh.shape["row"], mesh.shape["col"] * mesh.shape["section"])
    return jax.shard_map(body, mesh=mesh, in_specs=in_specs, out_specs=out_specs, check_vma=False)
```

```python
import functools

import jax
import jax.numpy as jnp
from jax import lax
from jax.experimental import pallas as pl
from jax.experimental.pallas import tpu as pltpu
from jax.sharding import PartitionSpec as P

PLANE = ("col", "section")
F32 = jnp.float32
BF16 = jnp.bfloat16


def mm(left, right):
    return jnp.dot(left, right, preferred_element_type=F32)


def mm_t(left, right):
    return lax.dot_general(left, right, (((1,), (1,)), ((), ())), preferred_element_type=F32)


def grad_kernel(places, tile, *refs):
    out_ref, left, right, sems = refs[-4:]
    pieces = refs[:-4]

    @pl.when(pl.program_id(0) == 0)
    def load():
        copies = []
        for i, (piece, (side, row, column)) in enumerate(zip(pieces, places)):
            to = (left, right)[side].at[pl.ds(row, piece.shape[0]), pl.ds(column, piece.shape[1])]
            copies.append(pltpu.make_async_copy(piece, to, sems.at[i]))
        for copy in copies:
            copy.start()
        for copy in copies:
            copy.wait()

    columns = pl.ds(pl.multiple_of(pl.program_id(0) * tile, tile), tile)
    out_ref[...] = lax.dot_general(
        left[:, columns], right[...], (((0,), (0,)), ((), ())), preferred_element_type=F32
    )


def weight_grad(lefts, rights):
    places, pieces, shapes = [], [], []
    for side, grid in enumerate((lefts, rights)):
        row = 0
        for line in grid:
            column = 0
            for piece in line:
                places.append((side, row, column))
                pieces.append(piece)
                column += piece.shape[1]
            row += line[0].shape[0]
        shapes.append((row, column))
    (depth, m), (_, n) = shapes
    tile = 256 if m % 256 == 0 else 128
    return pl.pallas_call(
        functools.partial(grad_kernel, places, tile),
        grid=(m // tile,),
        in_specs=[pl.BlockSpec(memory_space=pl.ANY)] * len(pieces),
        out_specs=pl.BlockSpec((tile, n), lambda i: (i, 0)),
        out_shape=jax.ShapeDtypeStruct((m, n), F32),
        scratch_shapes=[
            pltpu.VMEM((depth, m), BF16),
            pltpu.VMEM((depth, n), BF16),
            pltpu.SemaphoreType.DMA((len(pieces),)),
        ],
        compiler_params=pltpu.CompilerParams(vmem_limit_bytes=14 << 20),
        cost_estimate=pl.CostEstimate(
            flops=2 * depth * m * n,
            bytes_accessed=2 * depth * (m + n) + 4 * m * n,
            transcendentals=0,
        ),
    )(*pieces)


def reverse_bits(value, width):
    out = 0
    for bit in range(width):
        out |= ((value >> bit) & 1) << (width - 1 - bit)
    return out


def after(value, earlier):
    first = earlier[(0,) * earlier.ndim]
    return jnp.where(first == first, value, jnp.zeros_like(value))


def halves(size):
    middle = -(-size // 256) * 128
    return [(0, middle), (middle, size)]


class Plane:
    def __init__(self, size):
        self.size = size
        self.width = (size // 2).bit_length() - 1
        assert 2 << self.width == size
        self.rev = [reverse_bits(k, self.width) for k in range(size // 2)]
        self.perms = []
        for step in range(self.width):
            even, odd = 2 << step, 2 << (self.width - 1 - step)
            self.perms.append([(c, c ^ (odd if c & 1 else even)) for c in range(size)])
        self.swap = [(c, c ^ 1) for c in range(size)]

    def gather(self, block):
        own = block
        for perm in self.perms:
            own = jnp.concatenate([own, lax.ppermute(own, PLANE, perm)], axis=0)
        return own, lax.ppermute(own, PLANE, self.swap)

    def scatter(self, full):
        b = full.shape[0] // self.size
        block = lambda i: full[i * b : (i + 1) * b]
        half = self.size // 2
        mine = jnp.concatenate([block(2 * k) for k in range(half)], axis=0)
        send = jnp.concatenate([block(2 * self.rev[k] + 1) for k in range(half)], axis=0)
        got = lax.ppermute(send, PLANE, self.swap)
        acc = mine.astype(F32) + got.astype(F32)
        for perm in reversed(self.perms):
            half = acc.shape[0] // 2
            got = lax.ppermute(acc[half:].astype(full.dtype), PLANE, perm)
            acc = acc[:half] + got.astype(F32)
        return acc

    def total(self, value):
        for perm in self.perms + [self.swap]:
            value = value + lax.ppermute(value, PLANE, perm)
        return value


class Rows:
    def __init__(self, size, plane):
        self.size = size
        self.ring = [(r, (r + 1) % size) for r in range(size)]
        self.me = lax.axis_index("row")
        c = lax.axis_index(PLANE)
        self.odd = (c & 1) == 1
        self.slots = []
        for back in range(size):
            k = (c >> 1) ^ lax.rem(self.me + (size - back), size)
            flipped = jnp.asarray(plane.rev, jnp.int32)[k]
            self.slots.append((jnp.where(self.odd, flipped, k), jnp.where(self.odd, k, flipped)))

    def parts(self, own, other):
        b = own.shape[0] // self.size
        return [
            [
                lax.dynamic_slice_in_dim(own, at * b, b, 0),
                lax.dynamic_slice_in_dim(other, at_other * b, b, 0),
            ]
            for at, at_other in self.slots
        ]

    def place(self, full, block, back):
        rows = block.shape[0]
        return lax.dynamic_update_slice_in_dim(full, block, self.slots[back][0] * rows, 0)

    def shift(self, value):
        return lax.ppermute(value, "row", self.ring)

    def reduce(self, parts, products):
        got, first = None, None
        for back in range(1, self.size + 1):
            rows = jnp.concatenate(parts[back % self.size], axis=0)
            sums = [product(rows) for product in products]
            if got is not None:
                sums = [s + g.astype(F32) for s, g in zip(sums, got)]
            if back < self.size:
                got = [self.shift(s.astype(BF16)) for s in sums]
                first = got[0] if first is None else first
        return sums, first

    def gather(self, blocks, product, beside=None):
        steps = [blocks]
        for back in range(1, self.size):
            sent = steps[-1]
            if back == 2 and beside is not None:
                sent = sent[:-1] + [after(sent[-1], beside)]
            steps.append([self.shift(b) for b in sent])
        made = [product(step) for step in steps]
        return steps, made, self.placed(made)

    def placed(self, blocks):
        out = jnp.zeros((blocks[0].shape[0] * self.size,) + blocks[0].shape[1:], blocks[0].dtype)
        for back, block in enumerate(blocks):
            out = self.place(out, block, back)
        return out

    def total(self, value):
        step = 1
        while step < self.size:
            value = value + lax.ppermute(value, "row", [(r, r ^ step) for r in range(self.size)])
            step *= 2
        return value

    def own_order(self, value):
        half = value.shape[0] // 2
        return jnp.where(self.odd, jnp.concatenate([value[half:], value[:half]], axis=0), value)


def lines(parts):
    return [[piece] for part in parts for piece in part]


def make_body(n_row, n_plane):
    plane = Plane(n_plane)
    assert n_plane == 2 * n_row

    def body(x, gain, gate_w, up_w, down_w, proj_w, teacher, loss_mask):
        rows = Rows(n_row, plane)
        block = x.shape[0]
        features = x.shape[1] * n_row

        own, other = plane.gather((x.astype(F32) * gain[None, :]).astype(BF16))
        scaled = rows.parts(own, other)
        (gate, up), moved = rows.reduce(scaled, [lambda a: mm(a, gate_w), lambda a: mm(a, up_w)])
        squares = [jnp.sum(jnp.square(p.astype(F32) / gain[None, :]), axis=1) for p in (own, other)]
        squares = rows.total(after(jnp.concatenate(squares), moved))
        inv_all = lax.rsqrt(squares / features + 1e-05)
        inv = jnp.concatenate(rows.parts(*jnp.split(inv_all, 2))[0])[:, None]

        target = lax.all_to_all(
            after(teacher, moved), PLANE, split_axis=1, concat_axis=0, tiled=True
        )
        target = rows.own_order(target).astype(F32)
        keep = rows.own_order(loss_mask.astype(F32))
        inv = after(inv, target)
        gate, up = gate * inv, up * inv
        sigma = jax.nn.sigmoid(gate)
        activated = gate * sigma
        hidden = (activated * up).astype(BF16)
        cuts = halves(hidden.shape[1])
        hiddens, _, ffn = rows.gather(
            [hidden[:, lo:hi] for lo, hi in cuts],
            lambda bs: sum(mm(b, down_w[lo:hi]) for b, (lo, hi) in zip(bs, cuts)).astype(BF16),
        )
        residual = (x.astype(F32) + plane.scatter(ffn)).astype(BF16)
        residuals = rows.parts(*plane.gather(residual))

        ecuts = halves(proj_w.shape[1])
        predicted, _ = rows.reduce(
            residuals, [lambda a, lo=lo, hi=hi: mm(a, proj_w[:, lo:hi]) for lo, hi in ecuts]
        )
        error = [p - target[:, lo:hi] for p, (lo, hi) in zip(predicted, ecuts)]
        masked = [e * keep[:, None] for e in error]

        pred_grads, _, back = rows.gather(
            [m.astype(BF16) for m in masked],
            lambda bs: sum(mm_t(b, proj_w[:, lo:hi]) for b, (lo, hi) in zip(bs, ecuts)).astype(BF16),
        )
        resid_grad = plane.scatter(back).astype(BF16)
        resid_grads = rows.parts(*plane.gather(resid_grad))

        hid_grad, _ = rows.reduce(
            resid_grads, [lambda a, lo=lo, hi=hi: mm_t(a, down_w[lo:hi]) for lo, hi in cuts]
        )
        hid_grad = jnp.concatenate(hid_grad, axis=1)
        gate_grad = hid_grad * up * (sigma * (1.0 + gate * (1.0 - sigma)))
        up_grad = hid_grad * activated
        blocks = [(gate_grad * inv).astype(BF16), (up_grad * inv).astype(BF16)]

        def held(parts):
            return [[after(p, blocks[1]) for p in parts[0]]] + parts[1:]

        grad_proj = weight_grad(lines(held(residuals)), pred_grads)
        grad_down = weight_grad(hiddens, lines(held(resid_grads)))
        grads, made, back = rows.gather(
            blocks,
            lambda b: (mm_t(b[0], gate_w) + mm_t(b[1], up_w)).astype(BF16),
            grad_proj[:1, :1] + grad_down[:1, :1],
        )
        normed_grad = plane.scatter(back)
        inner = jnp.sum(normed_grad * gain[None, :] * x.astype(F32), axis=1)
        loss_sum = 0.5 * sum(jnp.sum(m * e) for m, e in zip(masked, error))
        loss_parts = jnp.stack([loss_sum, jnp.sum(keep)])
        gain_sum = sum(
            jnp.sum(m.astype(F32) * jnp.concatenate(p, axis=0).astype(F32), axis=0)
            for m, p in zip(made, scaled)
        )
        sums = plane.total(jnp.concatenate([gain_sum / gain, loss_parts]))
        grad_gain = sums[:-2]
        sums = rows.total(jnp.concatenate([inner, sums[-2:]]))
        inner = sums[:-2]
        loss_value = sums[-2] / (sums[-1] / n_plane)

        grad_gate = weight_grad(lines(scaled), [g[:1] for g in grads])
        grad_up = weight_grad(lines(scaled), [g[1:] for g in grads])

        inv_own = inv_all[:block]
        grad_input = (
            resid_grad.astype(F32)
            + gain[None, :] * normed_grad
            - x.astype(F32) * (inv_own * inv_own * inner / features)[:, None]
        )
        return (loss_value, grad_gain, grad_gate, grad_up, grad_down, grad_proj, grad_input)

    return body


def solution(mesh):
    in_specs = (
        P(PLANE, "row"),
        P("row"),
        P("row", PLANE),
        P("row", PLANE),
        P(PLANE, "row"),
        P("row", PLANE),
        P(("row", "col", "section"), None),
        P("row"),
    )
    out_specs = (
        P(),
        P("row"),
        P("row", PLANE),
        P("row", PLANE),
        P(PLANE, "row"),
        P("row", PLANE),
        P(PLANE, "row"),
    )
    body = make_body(mesh.shape["row"], mesh.shape["col"] * mesh.shape["section"])
    return jax.shard_map(body, mesh=mesh, in_specs=in_specs, out_specs=out_specs, check_vma=False)
```

```python
import functools

import jax
import jax.numpy as jnp
from jax import lax
from jax.experimental import pallas as pl
from jax.experimental.pallas import tpu as pltpu
from jax.sharding import PartitionSpec as P

PLANE = ("col", "section")
F32 = jnp.float32
BF16 = jnp.bfloat16


def mm(left, right):
    return jnp.dot(left, right, preferred_element_type=F32)


def mm_t(left, right):
    return lax.dot_general(left, right, (((1,), (1,)), ((), ())), preferred_element_type=F32)


def grad_kernel(places, tile, *refs):
    pieces = refs[: len(places)]
    out_ref, _, left, right, sems = refs[-5:]

    @pl.when(pl.program_id(0) == 0)
    def load():
        copies = []
        for i, (piece, (side, row, column)) in enumerate(zip(pieces, places)):
            to = (left, right)[side].at[pl.ds(row, piece.shape[0]), pl.ds(column, piece.shape[1])]
            copies.append(pltpu.make_async_copy(piece, to, sems.at[i]))
        for copy in copies:
            copy.start()
        for copy in copies:
            copy.wait()

    columns = pl.ds(pl.multiple_of(pl.program_id(0) * tile, tile), tile)
    out_ref[...] = lax.dot_general(
        left[:, columns], right[...], (((0,), (0,)), ((), ())), preferred_element_type=F32
    )


def weight_grad(lefts, rights, through, *earlier):
    places, pieces, shapes = [], [], []
    for side, grid in enumerate((lefts, rights)):
        row = 0
        for line in grid:
            column = 0
            for piece in line:
                places.append((side, row, column))
                pieces.append(piece)
                column += piece.shape[1]
            row += line[0].shape[0]
        shapes.append((row, column))
    (depth, m), (_, n) = shapes
    tile = 256 if m % 256 == 0 else 128
    operands = pieces + list(earlier) + [through]
    return pl.pallas_call(
        functools.partial(grad_kernel, places, tile),
        grid=(m // tile,),
        in_specs=[pl.BlockSpec(memory_space=pl.ANY)] * len(operands),
        out_specs=[pl.BlockSpec((tile, n), lambda i: (i, 0)), pl.BlockSpec(memory_space=pl.ANY)],
        out_shape=[
            jax.ShapeDtypeStruct((m, n), F32),
            jax.ShapeDtypeStruct(through.shape, through.dtype),
        ],
        input_output_aliases={len(operands) - 1: 1},
        scratch_shapes=[
            pltpu.VMEM((depth, m), BF16),
            pltpu.VMEM((depth, n), BF16),
            pltpu.SemaphoreType.DMA((len(pieces),)),
        ],
        compiler_params=pltpu.CompilerParams(vmem_limit_bytes=14 << 20),
        cost_estimate=pl.CostEstimate(
            flops=2 * depth * m * n,
            bytes_accessed=2 * depth * (m + n) + 4 * m * n,
            transcendentals=0,
        ),
    )(*operands)


def reverse_bits(value, width):
    out = 0
    for bit in range(width):
        out |= ((value >> bit) & 1) << (width - 1 - bit)
    return out


def after(value, earlier):
    first = earlier[(0,) * earlier.ndim]
    return jnp.where(first == first, value, jnp.zeros_like(value))


def halves(size):
    middle = -(-size // 256) * 128
    return [(0, middle), (middle, size)]


class Plane:
    def __init__(self, size):
        self.size = size
        self.width = (size // 2).bit_length() - 1
        assert 2 << self.width == size
        self.rev = [reverse_bits(k, self.width) for k in range(size // 2)]
        self.perms = []
        for step in range(self.width):
            even, odd = 2 << step, 2 << (self.width - 1 - step)
            self.perms.append([(c, c ^ (odd if c & 1 else even)) for c in range(size)])
        self.swap = [(c, c ^ 1) for c in range(size)]

    def gather(self, block):
        own = block
        for perm in self.perms:
            own = jnp.concatenate([own, lax.ppermute(own, PLANE, perm)], axis=0)
        return own, lax.ppermute(own, PLANE, self.swap)

    def scatter(self, full, beside=()):
        b = full.shape[0] // self.size
        block = lambda i: full[i * b : (i + 1) * b]
        half = self.size // 2
        mine = jnp.concatenate([block(2 * k) for k in range(half)], axis=0)
        send = jnp.concatenate([block(2 * self.rev[k] + 1) for k in range(half)], axis=0)
        got = lax.ppermute(send, PLANE, self.swap)
        acc = mine.astype(F32) + got.astype(F32)
        for i, perm in enumerate(reversed(self.perms)):
            half = acc.shape[0] // 2
            kept, sent = acc[:half], acc[half:].astype(full.dtype)
            got = lax.ppermute(sent, PLANE, perm)
            if i < len(beside):
                kept = beside[i](kept, sent)
            acc = kept + got.astype(F32)
        return acc

    def total(self, value):
        for perm in self.perms + [self.swap]:
            value = value + lax.ppermute(value, PLANE, perm)
        return value


class Rows:
    def __init__(self, size, plane):
        self.size = size
        self.ring = [(r, (r + 1) % size) for r in range(size)]
        self.me = lax.axis_index("row")
        c = lax.axis_index(PLANE)
        self.odd = (c & 1) == 1
        self.slots = []
        for back in range(size):
            k = (c >> 1) ^ lax.rem(self.me + (size - back), size)
            flipped = jnp.asarray(plane.rev, jnp.int32)[k]
            self.slots.append((jnp.where(self.odd, flipped, k), jnp.where(self.odd, k, flipped)))

    def parts(self, own, other):
        b = own.shape[0] // self.size
        return [
            [
                lax.dynamic_slice_in_dim(own, at * b, b, 0),
                lax.dynamic_slice_in_dim(other, at_other * b, b, 0),
            ]
            for at, at_other in self.slots
        ]

    def place(self, full, block, back):
        rows = block.shape[0]
        return lax.dynamic_update_slice_in_dim(full, block, self.slots[back][0] * rows, 0)

    def shift(self, value):
        return lax.ppermute(value, "row", self.ring)

    def reduce(self, parts, products, beside=None):
        got, first = None, None
        for back in range(1, self.size + 1):
            rows = jnp.concatenate(parts[back % self.size], axis=0)
            sums = [product(rows) for product in products]
            if back == 2 and beside is not None:
                sums[-1] = beside(sums[-1], sent[-1])
            if got is not None:
                sums = [s + g.astype(F32) for s, g in zip(sums, got)]
            if back < self.size:
                sent = [s.astype(BF16) for s in sums]
                got = [self.shift(s) for s in sent]
                first = got[0] if first is None else first
        return sums, first

    def gather(self, blocks, product, beside=None):
        steps = [blocks]
        for back in range(1, self.size):
            sent = steps[-1]
            if back == 2 and beside is not None:
                sent = sent[:-1] + [after(sent[-1], beside)]
            steps.append([self.shift(b) for b in sent])
        made = [product(step) for step in steps]
        return steps, made, self.placed(made)

    def placed(self, blocks):
        out = jnp.zeros((blocks[0].shape[0] * self.size,) + blocks[0].shape[1:], blocks[0].dtype)
        for back, block in enumerate(blocks):
            out = self.place(out, block, back)
        return out

    def sum_direct(self, value):
        total = value
        for step in range(1, self.size):
            total = total + lax.ppermute(
                value, "row", [(r, r ^ step) for r in range(self.size)]
            )
        return total

    def total(self, value):
        step = 1
        while step < self.size:
            value = value + lax.ppermute(value, "row", [(r, r ^ step) for r in range(self.size)])
            step *= 2
        return value

    def own_order(self, value):
        half = value.shape[0] // 2
        return jnp.where(self.odd, jnp.concatenate([value[half:], value[:half]], axis=0), value)


def lines(parts):
    return [[piece] for part in parts for piece in part]


def make_body(n_row, n_plane):
    plane = Plane(n_plane)
    assert n_plane == 2 * n_row

    def body(x, gain, gate_w, up_w, down_w, proj_w, teacher, loss_mask):
        rows = Rows(n_row, plane)
        block = x.shape[0]
        features = x.shape[1] * n_row

        own, other = plane.gather((x.astype(F32) * gain[None, :]).astype(BF16))
        scaled = rows.parts(own, other)
        (gate, up), moved = rows.reduce(scaled, [lambda a: mm(a, gate_w), lambda a: mm(a, up_w)])
        squares = [jnp.sum(jnp.square(p.astype(F32) / gain[None, :]), axis=1) for p in (own, other)]
        squares = rows.sum_direct(after(jnp.concatenate(squares), moved))
        inv_all = lax.rsqrt(squares / features + 1e-05)
        inv = jnp.concatenate(rows.parts(*jnp.split(inv_all, 2))[0])[:, None]

        target = lax.all_to_all(
            after(teacher, moved), PLANE, split_axis=1, concat_axis=0, tiled=True
        )
        target = rows.own_order(target).astype(F32)
        keep = rows.own_order(loss_mask.astype(F32))
        inv = after(inv, target)
        gate, up = gate * inv, up * inv
        sigma = jax.nn.sigmoid(gate)
        activated = gate * sigma
        hidden = (activated * up).astype(BF16)
        cuts = halves(hidden.shape[1])
        hiddens, _, ffn = rows.gather(
            [hidden[:, lo:hi] for lo, hi in cuts],
            lambda bs: sum(mm(b, down_w[lo:hi]) for b, (lo, hi) in zip(bs, cuts)).astype(BF16),
        )
        residual = (x.astype(F32) + plane.scatter(ffn)).astype(BF16)
        residuals = rows.parts(*plane.gather(residual))

        ecuts = halves(proj_w.shape[1])
        predicted, _ = rows.reduce(
            residuals, [lambda a, lo=lo, hi=hi: mm(a, proj_w[:, lo:hi]) for lo, hi in ecuts]
        )
        error = [p - target[:, lo:hi] for p, (lo, hi) in zip(predicted, ecuts)]
        masked = [e * keep[:, None] for e in error]

        pred_grads, _, back = rows.gather(
            [m.astype(BF16) for m in masked],
            lambda bs: sum(mm_t(b, proj_w[:, lo:hi]) for b, (lo, hi) in zip(bs, ecuts)).astype(BF16),
        )
        resid_grad = plane.scatter(back).astype(BF16)
        resid_grads = rows.parts(*plane.gather(resid_grad))

        found = {}

        def grad(name, lefts, rights, through, *earlier):
            found[name], through = weight_grad(lefts, rights, through, *earlier)
            return through

        hid_grad, _ = rows.reduce(
            resid_grads,
            [lambda a, lo=lo, hi=hi: mm_t(a, down_w[lo:hi]) for lo, hi in cuts],
            lambda own, sent: grad("down", hiddens, lines(resid_grads), own, sent),
        )
        hid_grad = jnp.concatenate(hid_grad, axis=1)
        gate_grad = hid_grad * up * (sigma * (1.0 + gate * (1.0 - sigma)))
        up_grad = hid_grad * activated
        blocks = [(gate_grad * inv).astype(BF16), (up_grad * inv).astype(BF16)]

        last = grad("proj", lines(residuals), pred_grads, keep, blocks[1])
        grads, made, back = rows.gather(
            blocks,
            lambda b: (mm_t(b[0], gate_w) + mm_t(b[1], up_w)).astype(BF16),
            last,
        )
        gates, ups = [g[:1] for g in grads], [g[1:] for g in grads]
        normed_grad = plane.scatter(
            back,
            (
                lambda kept, sent: grad("gate", lines(scaled), gates, kept, sent),
                lambda kept, sent: grad("up", lines(scaled), ups, kept, sent),
            ),
        )
        inner = jnp.sum(normed_grad * gain[None, :] * x.astype(F32), axis=1)
        loss_sum = 0.5 * sum(jnp.sum(m * e) for m, e in zip(masked, error))
        loss_parts = jnp.stack([loss_sum, jnp.sum(last)])
        gain_sum = sum(
            jnp.sum(m.astype(F32) * jnp.concatenate(p, axis=0).astype(F32), axis=0)
            for m, p in zip(made, scaled)
        )
        sums = plane.total(jnp.concatenate([gain_sum / gain, loss_parts]))
        grad_gain = sums[:-2]
        sums = rows.total(jnp.concatenate([inner, sums[-2:]]))
        inner = sums[:-2]
        loss_value = sums[-2] / (sums[-1] / n_plane)

        inv_own = inv_all[:block]
        grad_input = (
            resid_grad.astype(F32)
            + gain[None, :] * normed_grad
            - x.astype(F32) * (inv_own * inv_own * inner / features)[:, None]
        )
        return (
            loss_value,
            grad_gain,
            found["gate"],
            found["up"],
            found["down"],
            found["proj"],
            grad_input,
        )

    return body


def solution(mesh):
    in_specs = (
        P(PLANE, "row"),
        P("row"),
        P("row", PLANE),
        P("row", PLANE),
        P(PLANE, "row"),
        P("row", PLANE),
        P(("row", "col", "section"), None),
        P("row"),
    )
    out_specs = (
        P(),
        P("row"),
        P("row", PLANE),
        P("row", PLANE),
        P(PLANE, "row"),
        P("row", PLANE),
        P(PLANE, "row"),
    )
    body = make_body(mesh.shape["row"], mesh.shape["col"] * mesh.shape["section"])
    return jax.shard_map(body, mesh=mesh, in_specs=in_specs, out_specs=out_specs, check_vma=False)
```

```python
import functools

import jax
import jax.numpy as jnp
from jax import lax
from jax.experimental import pallas as pl
from jax.experimental.pallas import tpu as pltpu
from jax.sharding import PartitionSpec as P

PLANE = ("col", "section")
F32 = jnp.float32
BF16 = jnp.bfloat16


def mm(left, right):
    return jnp.dot(left, right, preferred_element_type=F32)


def mm_t(left, right):
    return lax.dot_general(left, right, (((1,), (1,)), ((), ())), preferred_element_type=F32)


def grad_kernel(places, n_inputs, tile, *refs):
    pieces, out_ref = refs[: len(places)], refs[n_inputs]
    left, right, sems = refs[-3:]

    @pl.when(pl.program_id(0) == 0)
    def load():
        copies = []
        for i, (piece, (side, row, column)) in enumerate(zip(pieces, places)):
            to = (left, right)[side].at[pl.ds(row, piece.shape[0]), pl.ds(column, piece.shape[1])]
            copies.append(pltpu.make_async_copy(piece, to, sems.at[i]))
        for copy in copies:
            copy.start()
        for copy in copies:
            copy.wait()

    columns = pl.ds(pl.multiple_of(pl.program_id(0) * tile, tile), tile)
    out_ref[...] = lax.dot_general(
        left[:, columns], right[...], (((0,), (0,)), ((), ())), preferred_element_type=F32
    )


def weight_grad(lefts, rights, through, *earlier):
    places, pieces, shapes = [], [], []
    for side, grid in enumerate((lefts, rights)):
        row = 0
        for line in grid:
            column = 0
            for piece in line:
                places.append((side, row, column))
                pieces.append(piece)
                column += piece.shape[1]
            row += line[0].shape[0]
        shapes.append((row, column))
    (depth, m), (_, n) = shapes
    tile = 256 if m % 256 == 0 else 128
    operands = pieces + list(earlier) + list(through)
    first = len(operands) - len(through)
    made, *through = pl.pallas_call(
        functools.partial(grad_kernel, places, len(operands), tile),
        grid=(m // tile,),
        in_specs=[pl.BlockSpec(memory_space=pl.ANY)] * len(operands),
        out_specs=[pl.BlockSpec((tile, n), lambda i: (i, 0))]
        + [pl.BlockSpec(memory_space=pl.ANY)] * len(through),
        out_shape=[jax.ShapeDtypeStruct((m, n), F32)]
        + [jax.ShapeDtypeStruct(a.shape, a.dtype) for a in through],
        input_output_aliases={first + i: 1 + i for i in range(len(through))},
        scratch_shapes=[
            pltpu.VMEM((depth, m), BF16),
            pltpu.VMEM((depth, n), BF16),
            pltpu.SemaphoreType.DMA((len(pieces),)),
        ],
        compiler_params=pltpu.CompilerParams(vmem_limit_bytes=14 << 20),
        cost_estimate=pl.CostEstimate(
            flops=2 * depth * m * n,
            bytes_accessed=2 * depth * (m + n) + 4 * m * n,
            transcendentals=0,
        ),
    )(*operands)
    return made, through


def reverse_bits(value, width):
    out = 0
    for bit in range(width):
        out |= ((value >> bit) & 1) << (width - 1 - bit)
    return out


def after(value, earlier):
    first = earlier[(0,) * earlier.ndim]
    return jnp.where(first == first, value, jnp.zeros_like(value))


def halves(size):
    middle = -(-size // 256) * 128
    return [(0, middle), (middle, size)]


class Plane:
    def __init__(self, size):
        self.size = size
        self.width = (size // 2).bit_length() - 1
        assert 2 << self.width == size
        self.rev = [reverse_bits(k, self.width) for k in range(size // 2)]
        self.perms = []
        for step in range(self.width):
            even, odd = 2 << step, 2 << (self.width - 1 - step)
            self.perms.append([(c, c ^ (odd if c & 1 else even)) for c in range(size)])
        self.swap = [(c, c ^ 1) for c in range(size)]

    def gather(self, block):
        own = block
        for perm in self.perms:
            own = jnp.concatenate([own, lax.ppermute(own, PLANE, perm)], axis=0)
        return own, lax.ppermute(own, PLANE, self.swap)

    def scatter(self, full, beside=()):
        b = full.shape[0] // self.size
        block = lambda i: full[i * b : (i + 1) * b]
        half = self.size // 2
        mine = jnp.concatenate([block(2 * k) for k in range(half)], axis=0)
        send = jnp.concatenate([block(2 * self.rev[k] + 1) for k in range(half)], axis=0)
        got = lax.ppermute(send, PLANE, self.swap)
        acc = mine.astype(F32) + got.astype(F32)
        for i, perm in enumerate(reversed(self.perms)):
            half = acc.shape[0] // 2
            kept, sent = acc[:half], acc[half:].astype(full.dtype)
            got = lax.ppermute(sent, PLANE, perm)
            if i < len(beside):
                (kept,) = beside[i]([kept], sent)
            acc = kept + got.astype(F32)
        return acc

    def sum_direct(self, value):
        value = value + lax.ppermute(value, PLANE, self.swap)
        total = value
        for chip in range(2, self.size, 2):
            perm = [(c, c ^ chip) for c in range(self.size)]
            total = total + lax.ppermute(value, PLANE, perm)
        return total


class Rows:
    def __init__(self, size, plane):
        self.size = size
        self.ring = [(r, (r + 1) % size) for r in range(size)]
        self.me = lax.axis_index("row")
        c = lax.axis_index(PLANE)
        self.odd = (c & 1) == 1
        self.slots = []
        for back in range(size):
            k = (c >> 1) ^ lax.rem(self.me + (size - back), size)
            flipped = jnp.asarray(plane.rev, jnp.int32)[k]
            self.slots.append((jnp.where(self.odd, flipped, k), jnp.where(self.odd, k, flipped)))

    def parts(self, own, other):
        b = own.shape[0] // self.size
        return [
            [
                lax.dynamic_slice_in_dim(own, at * b, b, 0),
                lax.dynamic_slice_in_dim(other, at_other * b, b, 0),
            ]
            for at, at_other in self.slots
        ]

    def place(self, full, block, back):
        rows = block.shape[0]
        return lax.dynamic_update_slice_in_dim(full, block, self.slots[back][0] * rows, 0)

    def shift(self, value):
        return lax.ppermute(value, "row", self.ring)

    def reduce(self, parts, products, beside=None):
        got, first = None, None
        for back in range(1, self.size + 1):
            rows = jnp.concatenate(parts[back % self.size], axis=0)
            sums = [product(rows) for product in products]
            if back == 2 and beside is not None:
                (sums[-1],) = beside([sums[-1]], sent[-1])
            if got is not None:
                sums = [s + g.astype(F32) for s, g in zip(sums, got)]
            if back < self.size:
                sent = [s.astype(BF16) for s in sums]
                got = [self.shift(s) for s in sent]
                first = got[0] if first is None else first
        return sums, first

    def gather(self, blocks, product):
        steps = [blocks]
        for back in range(1, self.size):
            steps.append([self.shift(b) for b in steps[-1]])
        made = [product(step) for step in steps]
        return steps, made, self.placed(made)

    def placed(self, blocks):
        out = jnp.zeros((blocks[0].shape[0] * self.size,) + blocks[0].shape[1:], blocks[0].dtype)
        for back, block in enumerate(blocks):
            out = self.place(out, block, back)
        return out

    def sum_direct(self, value):
        total = value
        for step in range(1, self.size):
            total = total + lax.ppermute(
                value, "row", [(r, r ^ step) for r in range(self.size)]
            )
        return total

    def own_order(self, value):
        half = value.shape[0] // 2
        return jnp.where(self.odd, jnp.concatenate([value[half:], value[:half]], axis=0), value)


def lines(parts):
    return [[piece] for part in parts for piece in part]


def make_body(n_row, n_plane):
    plane = Plane(n_plane)
    assert n_plane == 2 * n_row

    def body(x, gain, gate_w, up_w, down_w, proj_w, teacher, loss_mask):
        rows = Rows(n_row, plane)
        block = x.shape[0]
        features = x.shape[1] * n_row

        own, other = plane.gather((x.astype(F32) * gain[None, :]).astype(BF16))
        scaled = rows.parts(own, other)
        (gate, up), moved = rows.reduce(scaled, [lambda a: mm(a, gate_w), lambda a: mm(a, up_w)])
        squares = [jnp.sum(jnp.square(p.astype(F32) / gain[None, :]), axis=1) for p in (own, other)]
        squares = rows.sum_direct(after(jnp.concatenate(squares), moved))
        inv_all = lax.rsqrt(squares / features + 1e-05)
        inv = jnp.concatenate(rows.parts(*jnp.split(inv_all, 2))[0])[:, None]

        target = lax.all_to_all(
            after(teacher, moved), PLANE, split_axis=1, concat_axis=0, tiled=True
        )
        target = rows.own_order(target).astype(F32)
        keep = rows.own_order(loss_mask.astype(F32))
        inv = after(inv, target)
        gate, up = gate * inv, up * inv
        sigma = jax.nn.sigmoid(gate)
        activated = gate * sigma
        hidden = (activated * up).astype(BF16)
        cuts = halves(hidden.shape[1])
        hiddens, _, ffn = rows.gather(
            [hidden[:, lo:hi] for lo, hi in cuts],
            lambda bs: sum(mm(b, down_w[lo:hi]) for b, (lo, hi) in zip(bs, cuts)).astype(BF16),
        )
        residual = (x.astype(F32) + plane.scatter(ffn)).astype(BF16)
        residuals = rows.parts(*plane.gather(residual))

        ecuts = halves(proj_w.shape[1])
        predicted, _ = rows.reduce(
            residuals, [lambda a, lo=lo, hi=hi: mm(a, proj_w[:, lo:hi]) for lo, hi in ecuts]
        )
        error = [p - target[:, lo:hi] for p, (lo, hi) in zip(predicted, ecuts)]
        masked = [e * keep[:, None] for e in error]

        pred_grads, _, back = rows.gather(
            [m.astype(BF16) for m in masked],
            lambda bs: sum(mm_t(b, proj_w[:, lo:hi]) for b, (lo, hi) in zip(bs, ecuts)).astype(BF16),
        )
        found = {}

        def grad(name, lefts, rights, through, *earlier):
            found[name], through = weight_grad(lefts, rights, through, *earlier)
            return through

        resid_grad = plane.scatter(
            back,
            [lambda kept, sent: grad("proj", lines(residuals), pred_grads, kept, sent)],
        ).astype(BF16)
        resid_grads = rows.parts(*plane.gather(resid_grad))

        hid_grad, _ = rows.reduce(
            resid_grads,
            [lambda a, lo=lo, hi=hi: mm_t(a, down_w[lo:hi]) for lo, hi in cuts],
            lambda own, sent: grad("down", hiddens, lines(resid_grads), own, sent),
        )
        hid_grad = jnp.concatenate(hid_grad, axis=1)
        gate_grad = hid_grad * up * (sigma * (1.0 + gate * (1.0 - sigma)))
        up_grad = hid_grad * activated
        blocks = [(gate_grad * inv).astype(BF16), (up_grad * inv).astype(BF16)]

        grads, made, back = rows.gather(
            blocks,
            lambda b: (mm_t(b[0], gate_w) + mm_t(b[1], up_w)).astype(BF16),
        )
        gates, ups = [g[:1] for g in grads], [g[1:] for g in grads]
        loss_sum = 0.5 * sum(jnp.sum(m * e) for m, e in zip(masked, error))
        gain_sum = sum(
            jnp.sum(m.astype(F32) * jnp.concatenate(p, axis=0).astype(F32), axis=0)
            for m, p in zip(made, scaled)
        )
        normed_grad = plane.scatter(
            back,
            [
                lambda kept, sent: grad("gate", lines(scaled), gates, kept, sent),
                lambda kept, sent: grad("up", lines(scaled), ups, kept, sent),
            ],
        )
        sums = jnp.concatenate([gain_sum / gain, jnp.stack([loss_sum, jnp.sum(keep)])])
        sums = plane.sum_direct(sums)
        grad_gain = sums[:-2]
        inner = jnp.sum(normed_grad * gain[None, :] * x.astype(F32), axis=1)
        sums = rows.sum_direct(jnp.concatenate([inner, sums[-2:]]))
        inner = sums[:-2]
        loss_value = sums[-2] / (sums[-1] / n_plane)

        inv_own = inv_all[:block]
        grad_input = (
            resid_grad.astype(F32)
            + gain[None, :] * normed_grad
            - x.astype(F32) * (inv_own * inv_own * inner / features)[:, None]
        )
        return (
            loss_value,
            grad_gain,
            found["gate"],
            found["up"],
            found["down"],
            found["proj"],
            grad_input,
        )

    return body


def solution(mesh):
    in_specs = (
        P(PLANE, "row"),
        P("row"),
        P("row", PLANE),
        P("row", PLANE),
        P(PLANE, "row"),
        P("row", PLANE),
        P(("row", "col", "section"), None),
        P("row"),
    )
    out_specs = (
        P(),
        P("row"),
        P("row", PLANE),
        P("row", PLANE),
        P(PLANE, "row"),
        P("row", PLANE),
        P(PLANE, "row"),
    )
    body = make_body(mesh.shape["row"], mesh.shape["col"] * mesh.shape["section"])
    return jax.shard_map(body, mesh=mesh, in_specs=in_specs, out_specs=out_specs, check_vma=False)
```

```python
import functools

import jax
import jax.numpy as jnp
from jax import lax
from jax.experimental import pallas as pl
from jax.experimental.pallas import tpu as pltpu
from jax.sharding import PartitionSpec as P

PLANE = ("col", "section")
F32 = jnp.float32
BF16 = jnp.bfloat16


def mm(left, right):
    return jnp.dot(left, right, preferred_element_type=F32)


def mm_t(left, right):
    return lax.dot_general(left, right, (((1,), (1,)), ((), ())), preferred_element_type=F32)


def grad_kernel(places, n_inputs, tile, *refs):
    pieces, out_ref = refs[: len(places)], refs[n_inputs]
    left, right, sems = refs[-3:]

    @pl.when(pl.program_id(0) == 0)
    def load():
        copies = []
        for i, (piece, (side, row, column)) in enumerate(zip(pieces, places)):
            to = (left, right)[side].at[pl.ds(row, piece.shape[0]), pl.ds(column, piece.shape[1])]
            copies.append(pltpu.make_async_copy(piece, to, sems.at[i]))
        for copy in copies:
            copy.start()
        for copy in copies:
            copy.wait()

    columns = pl.ds(pl.multiple_of(pl.program_id(0) * tile, tile), tile)
    out_ref[...] = lax.dot_general(
        left[:, columns], right[...], (((0,), (0,)), ((), ())), preferred_element_type=F32
    )


def weight_grad(lefts, rights, through, *earlier):
    places, pieces, shapes = [], [], []
    for side, grid in enumerate((lefts, rights)):
        row = 0
        for line in grid:
            column = 0
            for piece in line:
                places.append((side, row, column))
                pieces.append(piece)
                column += piece.shape[1]
            row += line[0].shape[0]
        shapes.append((row, column))
    (depth, m), (_, n) = shapes
    tile = 256 if m % 256 == 0 else 128
    operands = pieces + list(earlier) + list(through)
    first = len(operands) - len(through)
    made, *through = pl.pallas_call(
        functools.partial(grad_kernel, places, len(operands), tile),
        grid=(m // tile,),
        in_specs=[pl.BlockSpec(memory_space=pl.ANY)] * len(operands),
        out_specs=[pl.BlockSpec((tile, n), lambda i: (i, 0))]
        + [pl.BlockSpec(memory_space=pl.ANY)] * len(through),
        out_shape=[jax.ShapeDtypeStruct((m, n), F32)]
        + [jax.ShapeDtypeStruct(a.shape, a.dtype) for a in through],
        input_output_aliases={first + i: 1 + i for i in range(len(through))},
        scratch_shapes=[
            pltpu.VMEM((depth, m), BF16),
            pltpu.VMEM((depth, n), BF16),
            pltpu.SemaphoreType.DMA((len(pieces),)),
        ],
        compiler_params=pltpu.CompilerParams(vmem_limit_bytes=14 << 20),
        cost_estimate=pl.CostEstimate(
            flops=2 * depth * m * n,
            bytes_accessed=2 * depth * (m + n) + 4 * m * n,
            transcendentals=0,
        ),
    )(*operands)
    return made, through


def reverse_bits(value, width):
    out = 0
    for bit in range(width):
        out |= ((value >> bit) & 1) << (width - 1 - bit)
    return out


def after(value, earlier):
    first = earlier[(0,) * earlier.ndim]
    return jnp.where(first == first, value, jnp.zeros_like(value))


def halves(size):
    middle = -(-size // 256) * 128
    return [(0, middle), (middle, size)]


class Plane:
    def __init__(self, size):
        self.size = size
        self.width = (size // 2).bit_length() - 1
        assert 2 << self.width == size
        self.rev = [reverse_bits(k, self.width) for k in range(size // 2)]
        self.perms = []
        for step in range(self.width):
            even, odd = 2 << step, 2 << (self.width - 1 - step)
            self.perms.append([(c, c ^ (odd if c & 1 else even)) for c in range(size)])
        self.swap = [(c, c ^ 1) for c in range(size)]

    def partner(self, block):
        return lax.ppermute(block, PLANE, self.perms[0])

    def gather(self, block, paired=False):
        own = block
        for perm in self.perms[1:] if paired else self.perms:
            own = jnp.concatenate([own, lax.ppermute(own, PLANE, perm)], axis=0)
        return own, lax.ppermute(own, PLANE, self.swap)

    def scatter(self, full, beside=(), paired=False):
        b = full.shape[0] // self.size
        block = lambda i: full[i * b : (i + 1) * b]
        half = self.size // 2
        mine = jnp.concatenate([block(2 * k) for k in range(half)], axis=0)
        send = jnp.concatenate([block(2 * self.rev[k] + 1) for k in range(half)], axis=0)
        got = lax.ppermute(send, PLANE, self.swap)
        acc = mine.astype(F32) + got.astype(F32)
        for i, perm in enumerate(reversed(self.perms)):
            if paired and i == len(self.perms) - 1:
                sent = acc.astype(full.dtype)
                got = lax.ppermute(sent, PLANE, perm)
                middle = acc.shape[0] // 2
                got = jnp.concatenate([got[middle:], got[:middle]], axis=0)
                return sent.astype(F32) + got.astype(F32)
            half = acc.shape[0] // 2
            kept, sent = acc[:half], acc[half:].astype(full.dtype)
            got = lax.ppermute(sent, PLANE, perm)
            if i < len(beside):
                (kept,) = beside[i]([kept], sent)
            acc = kept + got.astype(F32)
        return acc

    def sum_direct(self, value):
        value = value + lax.ppermute(value, PLANE, self.swap)
        total = value
        for chip in range(2, self.size, 2):
            perm = [(c, c ^ chip) for c in range(self.size)]
            total = total + lax.ppermute(value, PLANE, perm)
        return total


class Rows:
    def __init__(self, size, plane):
        self.size = size
        self.ring = [(r, (r + 1) % size) for r in range(size)]
        self.me = lax.axis_index("row")
        c = lax.axis_index(PLANE)
        self.odd = (c & 1) == 1
        self.slots = []
        for back in range(size):
            k = (c >> 1) ^ lax.rem(self.me + (size - back), size)
            flipped = jnp.asarray(plane.rev, jnp.int32)[k]
            self.slots.append((jnp.where(self.odd, flipped, k), jnp.where(self.odd, k, flipped)))

    def parts(self, own, other):
        b = own.shape[0] // self.size
        return [
            [
                lax.dynamic_slice_in_dim(own, at * b, b, 0),
                lax.dynamic_slice_in_dim(other, at_other * b, b, 0),
            ]
            for at, at_other in self.slots
        ]

    def place(self, full, block, back):
        rows = block.shape[0]
        return lax.dynamic_update_slice_in_dim(full, block, self.slots[back][0] * rows, 0)

    def shift(self, value):
        return lax.ppermute(value, "row", self.ring)

    def reduce(self, parts, products, beside=None):
        got, first = None, None
        for back in range(1, self.size + 1):
            rows = jnp.concatenate(parts[back % self.size], axis=0)
            sums = [product(rows) for product in products]
            if back == 2 and beside is not None:
                (sums[-1],) = beside([sums[-1]], sent[-1])
            if got is not None:
                sums = [s + g.astype(F32) for s, g in zip(sums, got)]
            if back < self.size:
                sent = [s.astype(BF16) for s in sums]
                got = [self.shift(s) for s in sent]
                first = got[0] if first is None else first
        return sums, first

    def gather(self, blocks, product):
        steps = [blocks]
        for back in range(1, self.size):
            steps.append([self.shift(b) for b in steps[-1]])
        made = [product(step) for step in steps]
        return steps, made, self.placed(made)

    def placed(self, blocks):
        out = jnp.zeros((blocks[0].shape[0] * self.size,) + blocks[0].shape[1:], blocks[0].dtype)
        for back, block in enumerate(blocks):
            out = self.place(out, block, back)
        return out

    def sum_direct(self, value):
        total = value
        for step in range(1, self.size):
            total = total + lax.ppermute(
                value, "row", [(r, r ^ step) for r in range(self.size)]
            )
        return total

    def own_order(self, value):
        half = value.shape[0] // 2
        return jnp.where(self.odd, jnp.concatenate([value[half:], value[:half]], axis=0), value)


def lines(parts):
    return [[piece] for part in parts for piece in part]


def make_body(n_row, n_plane):
    plane = Plane(n_plane)
    assert n_plane == 2 * n_row

    def body(x, gain, gate_w, up_w, down_w, proj_w, teacher, loss_mask):
        rows = Rows(n_row, plane)
        block = x.shape[0]
        features = x.shape[1] * n_row

        own, other = plane.gather((x.astype(F32) * gain[None, :]).astype(BF16))
        scaled = rows.parts(own, other)
        (gate, up), moved = rows.reduce(scaled, [lambda a: mm(a, gate_w), lambda a: mm(a, up_w)])
        squares = [jnp.sum(jnp.square(p.astype(F32) / gain[None, :]), axis=1) for p in (own, other)]
        squares = rows.sum_direct(after(jnp.concatenate(squares), moved))
        inv_all = lax.rsqrt(squares / features + 1e-05)
        inv = jnp.concatenate(rows.parts(*jnp.split(inv_all, 2))[0])[:, None]

        target = lax.all_to_all(
            after(teacher, moved), PLANE, split_axis=1, concat_axis=0, tiled=True
        )
        target = rows.own_order(target).astype(F32)
        keep = rows.own_order(loss_mask.astype(F32))
        x_other = plane.partner(after(x, moved))
        inv = after(after(inv, target), x_other)
        gate, up = gate * inv, up * inv
        sigma = jax.nn.sigmoid(gate)
        activated = gate * sigma
        hidden = (activated * up).astype(BF16)
        cuts = halves(hidden.shape[1])
        hiddens, _, ffn = rows.gather(
            [hidden[:, lo:hi] for lo, hi in cuts],
            lambda bs: sum(mm(b, down_w[lo:hi]) for b, (lo, hi) in zip(bs, cuts)).astype(BF16),
        )
        x_pair = jnp.concatenate([x, x_other], axis=0)
        residual = (x_pair.astype(F32) + plane.scatter(ffn, paired=True)).astype(BF16)
        residuals = rows.parts(*plane.gather(residual, paired=True))

        ecuts = halves(proj_w.shape[1])
        predicted, _ = rows.reduce(
            residuals, [lambda a, lo=lo, hi=hi: mm(a, proj_w[:, lo:hi]) for lo, hi in ecuts]
        )
        error = [p - target[:, lo:hi] for p, (lo, hi) in zip(predicted, ecuts)]
        masked = [e * keep[:, None] for e in error]

        pred_grads, _, back = rows.gather(
            [m.astype(BF16) for m in masked],
            lambda bs: sum(mm_t(b, proj_w[:, lo:hi]) for b, (lo, hi) in zip(bs, ecuts)).astype(BF16),
        )
        found = {}

        def grad(name, lefts, rights, through, *earlier):
            found[name], through = weight_grad(lefts, rights, through, *earlier)
            return through

        resid_grad = plane.scatter(
            back,
            [lambda kept, sent: grad("proj", lines(residuals), pred_grads, kept, sent)],
            paired=True,
        ).astype(BF16)
        resid_grads = rows.parts(*plane.gather(resid_grad, paired=True))

        hid_grad, _ = rows.reduce(
            resid_grads,
            [lambda a, lo=lo, hi=hi: mm_t(a, down_w[lo:hi]) for lo, hi in cuts],
            lambda own, sent: grad("down", hiddens, lines(resid_grads), own, sent),
        )
        hid_grad = jnp.concatenate(hid_grad, axis=1)
        gate_grad = hid_grad * up * (sigma * (1.0 + gate * (1.0 - sigma)))
        up_grad = hid_grad * activated
        blocks = [(gate_grad * inv).astype(BF16), (up_grad * inv).astype(BF16)]

        grads, made, back = rows.gather(
            blocks,
            lambda b: (mm_t(b[0], gate_w) + mm_t(b[1], up_w)).astype(BF16),
        )
        gates, ups = [g[:1] for g in grads], [g[1:] for g in grads]
        loss_sum = 0.5 * sum(jnp.sum(m * e) for m, e in zip(masked, error))
        gain_sum = sum(
            jnp.sum(m.astype(F32) * jnp.concatenate(p, axis=0).astype(F32), axis=0)
            for m, p in zip(made, scaled)
        )
        normed_grad = plane.scatter(
            back,
            [
                lambda kept, sent: grad("gate", lines(scaled), gates, kept, sent),
                lambda kept, sent: grad("up", lines(scaled), ups, kept, sent),
            ],
        )
        sums = jnp.concatenate([gain_sum / gain, jnp.stack([loss_sum, jnp.sum(keep)])])
        sums = plane.sum_direct(sums)
        grad_gain = sums[:-2]
        inner = jnp.sum(normed_grad * gain[None, :] * x.astype(F32), axis=1)
        sums = rows.sum_direct(jnp.concatenate([inner, sums[-2:]]))
        inner = sums[:-2]
        loss_value = sums[-2] / (sums[-1] / n_plane)

        inv_own = inv_all[:block]
        grad_input = (
            resid_grad[:block].astype(F32)
            + gain[None, :] * normed_grad
            - x.astype(F32) * (inv_own * inv_own * inner / features)[:, None]
        )
        return (
            loss_value,
            grad_gain,
            found["gate"],
            found["up"],
            found["down"],
            found["proj"],
            grad_input,
        )

    return body


def solution(mesh):
    in_specs = (
        P(PLANE, "row"),
        P("row"),
        P("row", PLANE),
        P("row", PLANE),
        P(PLANE, "row"),
        P("row", PLANE),
        P(("row", "col", "section"), None),
        P("row"),
    )
    out_specs = (
        P(),
        P("row"),
        P("row", PLANE),
        P("row", PLANE),
        P(PLANE, "row"),
        P("row", PLANE),
        P(PLANE, "row"),
    )
    body = make_body(mesh.shape["row"], mesh.shape["col"] * mesh.shape["section"])
    return jax.shard_map(body, mesh=mesh, in_specs=in_specs, out_specs=out_specs, check_vma=False)
```

```python
import functools

import jax
import jax.numpy as jnp
from jax import lax
from jax.experimental import pallas as pl
from jax.experimental.pallas import tpu as pltpu
from jax.sharding import PartitionSpec as P

PLANE = ("col", "section")
F32 = jnp.float32
BF16 = jnp.bfloat16


def mm(left, right):
    return jnp.dot(left, right, preferred_element_type=F32)


def mm_t(left, right):
    return lax.dot_general(left, right, (((1,), (1,)), ((), ())), preferred_element_type=F32)


def grad_kernel(places, n_inputs, tile, *refs):
    pieces, out_ref = refs[: len(places)], refs[n_inputs]
    left, right, sems = refs[-3:]

    @pl.when(pl.program_id(0) == 0)
    def load():
        copies = []
        for i, (piece, (side, row, column)) in enumerate(zip(pieces, places)):
            to = (left, right)[side].at[pl.ds(row, piece.shape[0]), pl.ds(column, piece.shape[1])]
            copies.append(pltpu.make_async_copy(piece, to, sems.at[i]))
        for copy in copies:
            copy.start()
        for copy in copies:
            copy.wait()

    columns = pl.ds(pl.multiple_of(pl.program_id(0) * tile, tile), tile)
    out_ref[...] = lax.dot_general(
        left[:, columns], right[...], (((0,), (0,)), ((), ())), preferred_element_type=F32
    )


def weight_grad(lefts, rights, through, *earlier):
    places, pieces, shapes = [], [], []
    for side, grid in enumerate((lefts, rights)):
        row = 0
        for line in grid:
            column = 0
            for piece in line:
                places.append((side, row, column))
                pieces.append(piece)
                column += piece.shape[1]
            row += line[0].shape[0]
        shapes.append((row, column))
    (depth, m), (_, n) = shapes
    tile = next(t for t in (512, 256, 128) if m % t == 0)
    operands = pieces + list(earlier) + list(through)
    first = len(operands) - len(through)
    made, *through = pl.pallas_call(
        functools.partial(grad_kernel, places, len(operands), tile),
        grid=(m // tile,),
        in_specs=[pl.BlockSpec(memory_space=pl.ANY)] * len(operands),
        out_specs=[pl.BlockSpec((tile, n), lambda i: (i, 0))]
        + [pl.BlockSpec(memory_space=pl.ANY)] * len(through),
        out_shape=[jax.ShapeDtypeStruct((m, n), F32)]
        + [jax.ShapeDtypeStruct(a.shape, a.dtype) for a in through],
        input_output_aliases={first + i: 1 + i for i in range(len(through))},
        scratch_shapes=[
            pltpu.VMEM((depth, m), BF16),
            pltpu.VMEM((depth, n), BF16),
            pltpu.SemaphoreType.DMA((len(pieces),)),
        ],
        compiler_params=pltpu.CompilerParams(vmem_limit_bytes=16 << 20),
        cost_estimate=pl.CostEstimate(
            flops=2 * depth * m * n,
            bytes_accessed=2 * depth * (m + n) + 4 * m * n,
            transcendentals=0,
        ),
    )(*operands)
    return made, through


def reverse_bits(value, width):
    out = 0
    for bit in range(width):
        out |= ((value >> bit) & 1) << (width - 1 - bit)
    return out


def after(value, earlier):
    first = earlier[(0,) * earlier.ndim]
    return jnp.where(first == first, value, jnp.zeros_like(value))


def halves(size):
    middle = -(-size // 256) * 128
    return [(0, middle), (middle, size)]


class Plane:
    def __init__(self, size):
        self.size = size
        self.width = (size // 2).bit_length() - 1
        assert 2 << self.width == size
        self.rev = [reverse_bits(k, self.width) for k in range(size // 2)]
        self.perms = []
        for step in range(self.width):
            even, odd = 2 << step, 2 << (self.width - 1 - step)
            self.perms.append([(c, c ^ (odd if c & 1 else even)) for c in range(size)])
        self.swap = [(c, c ^ 1) for c in range(size)]

    def partner(self, block):
        return lax.ppermute(block, PLANE, self.perms[0])

    def gather(self, block, paired=False):
        own = block
        for perm in self.perms[1:] if paired else self.perms:
            own = jnp.concatenate([own, lax.ppermute(own, PLANE, perm)], axis=0)
        return own, lax.ppermute(own, PLANE, self.swap)

    def scatter(self, full, beside=(), paired=False):
        b = full.shape[0] // self.size
        block = lambda i: full[i * b : (i + 1) * b]
        half = self.size // 2
        mine = jnp.concatenate([block(2 * k) for k in range(half)], axis=0)
        send = jnp.concatenate([block(2 * self.rev[k] + 1) for k in range(half)], axis=0)
        got = lax.ppermute(send, PLANE, self.swap)
        acc = mine.astype(F32) + got.astype(F32)
        for i, perm in enumerate(reversed(self.perms)):
            if paired and i == len(self.perms) - 1:
                sent = acc.astype(full.dtype)
                got = lax.ppermute(sent, PLANE, perm)
                middle = acc.shape[0] // 2
                got = jnp.concatenate([got[middle:], got[:middle]], axis=0)
                return sent.astype(F32) + got.astype(F32)
            half = acc.shape[0] // 2
            kept, sent = acc[:half], acc[half:].astype(full.dtype)
            got = lax.ppermute(sent, PLANE, perm)
            if i < len(beside):
                (kept,) = beside[i]([kept], sent)
            acc = kept + got.astype(F32)
        return acc

    def sum_direct(self, value):
        value = value + lax.ppermute(value, PLANE, self.swap)
        total = value
        for chip in range(2, self.size, 2):
            perm = [(c, c ^ chip) for c in range(self.size)]
            total = total + lax.ppermute(value, PLANE, perm)
        return total


class Rows:
    def __init__(self, size, plane):
        self.size = size
        self.ring = [(r, (r + 1) % size) for r in range(size)]
        self.me = lax.axis_index("row")
        c = lax.axis_index(PLANE)
        self.odd = (c & 1) == 1
        self.slots = []
        for back in range(size):
            k = (c >> 1) ^ lax.rem(self.me + (size - back), size)
            flipped = jnp.asarray(plane.rev, jnp.int32)[k]
            self.slots.append((jnp.where(self.odd, flipped, k), jnp.where(self.odd, k, flipped)))

    def parts(self, own, other):
        b = own.shape[0] // self.size
        return [
            [
                lax.dynamic_slice_in_dim(own, at * b, b, 0),
                lax.dynamic_slice_in_dim(other, at_other * b, b, 0),
            ]
            for at, at_other in self.slots
        ]

    def place(self, full, block, back):
        rows = block.shape[0]
        return lax.dynamic_update_slice_in_dim(full, block, self.slots[back][0] * rows, 0)

    def shift(self, value):
        return lax.ppermute(value, "row", self.ring)

    def reduce(self, parts, products, beside=None):
        got, arrived = None, []
        for back in range(1, self.size + 1):
            rows = jnp.concatenate(parts[back % self.size], axis=0)
            sums = [product(rows) for product in products]
            if back == 2 and beside is not None:
                (sums[-1],) = beside([sums[-1]], sent[-1])
            if got is not None:
                sums = [s + g.astype(F32) for s, g in zip(sums, got)]
            if back < self.size:
                sent = [s.astype(BF16) for s in sums]
                got = [self.shift(s) for s in sent]
                arrived.append(got[-1])
        return sums, arrived

    def gather(self, blocks, product):
        steps = [blocks]
        for back in range(1, self.size):
            steps.append([self.shift(b) for b in steps[-1]])
        made = [product(step) for step in steps]
        return steps, made, self.placed(made)

    def placed(self, blocks):
        out = jnp.zeros((blocks[0].shape[0] * self.size,) + blocks[0].shape[1:], blocks[0].dtype)
        for back, block in enumerate(blocks):
            out = self.place(out, block, back)
        return out

    def sum_direct(self, value):
        total = value
        for step in range(1, self.size):
            total = total + lax.ppermute(
                value, "row", [(r, r ^ step) for r in range(self.size)]
            )
        return total

    def own_order(self, value):
        half = value.shape[0] // 2
        return jnp.where(self.odd, jnp.concatenate([value[half:], value[:half]], axis=0), value)


def lines(parts):
    return [[piece] for part in parts for piece in part]


def make_body(n_row, n_plane):
    plane = Plane(n_plane)
    assert n_plane == 2 * n_row

    def body(x, gain, gate_w, up_w, down_w, proj_w, teacher, loss_mask):
        rows = Rows(n_row, plane)
        block = x.shape[0]
        features = x.shape[1] * n_row

        own, other = plane.gather((x.astype(F32) * gain[None, :]).astype(BF16))
        scaled = rows.parts(own, other)
        (gate, up), moved = rows.reduce(scaled, [lambda a: mm(a, gate_w), lambda a: mm(a, up_w)])
        squares = [jnp.sum(jnp.square(p.astype(F32) / gain[None, :]), axis=1) for p in (own, other)]
        squares = rows.sum_direct(after(jnp.concatenate(squares), moved[0]))
        inv_all = lax.rsqrt(squares / features + 1e-05)
        inv = jnp.concatenate(rows.parts(*jnp.split(inv_all, 2))[0])[:, None]

        target = lax.all_to_all(
            after(teacher, moved[1]), PLANE, split_axis=1, concat_axis=0, tiled=True
        )
        target = rows.own_order(target).astype(F32)
        keep = rows.own_order(loss_mask.astype(F32))
        x_other = plane.partner(after(x, moved[0]))
        inv = after(after(inv, target), x_other)
        gate, up = gate * inv, up * inv
        sigma = jax.nn.sigmoid(gate)
        activated = gate * sigma
        hidden = (activated * up).astype(BF16)
        cuts = halves(hidden.shape[1])
        hiddens, _, ffn = rows.gather(
            [hidden[:, lo:hi] for lo, hi in cuts],
            lambda bs: sum(mm(b, down_w[lo:hi]) for b, (lo, hi) in zip(bs, cuts)).astype(BF16),
        )
        x_pair = jnp.concatenate([x, x_other], axis=0)
        residual = (x_pair.astype(F32) + plane.scatter(ffn, paired=True)).astype(BF16)
        residuals = rows.parts(*plane.gather(residual, paired=True))

        ecuts = halves(proj_w.shape[1])
        predicted, _ = rows.reduce(
            residuals, [lambda a, lo=lo, hi=hi: mm(a, proj_w[:, lo:hi]) for lo, hi in ecuts]
        )
        error = [p - target[:, lo:hi] for p, (lo, hi) in zip(predicted, ecuts)]
        masked = [e * keep[:, None] for e in error]

        pred_grads, _, back = rows.gather(
            [m.astype(BF16) for m in masked],
            lambda bs: sum(mm_t(b, proj_w[:, lo:hi]) for b, (lo, hi) in zip(bs, ecuts)).astype(BF16),
        )
        found = {}

        def grad(name, lefts, rights, through, *earlier):
            found[name], through = weight_grad(lefts, rights, through, *earlier)
            return through

        resid_grad = plane.scatter(
            back,
            [lambda kept, sent: grad("proj", lines(residuals), pred_grads, kept, sent)],
            paired=True,
        ).astype(BF16)
        resid_grads = rows.parts(*plane.gather(resid_grad, paired=True))

        hid_grad, _ = rows.reduce(
            resid_grads,
            [lambda a, lo=lo, hi=hi: mm_t(a, down_w[lo:hi]) for lo, hi in cuts],
            lambda own, sent: grad("down", hiddens, lines(resid_grads), own, sent),
        )
        hid_grad = jnp.concatenate(hid_grad, axis=1)
        gate_grad = hid_grad * up * (sigma * (1.0 + gate * (1.0 - sigma)))
        up_grad = hid_grad * activated
        blocks = [(gate_grad * inv).astype(BF16), (up_grad * inv).astype(BF16)]

        grads, made, back = rows.gather(
            blocks,
            lambda b: (mm_t(b[0], gate_w) + mm_t(b[1], up_w)).astype(BF16),
        )
        gates, ups = [g[:1] for g in grads], [g[1:] for g in grads]
        loss_sum = 0.5 * sum(jnp.sum(m * e) for m, e in zip(masked, error))
        gain_sum = sum(
            jnp.sum(m.astype(F32) * jnp.concatenate(p, axis=0).astype(F32), axis=0)
            for m, p in zip(made, scaled)
        )
        normed_grad = plane.scatter(
            back,
            [
                lambda kept, sent: grad("gate", lines(scaled), gates, kept, sent),
                lambda kept, sent: grad("up", lines(scaled), ups, kept, sent),
            ],
        )
        sums = jnp.concatenate([gain_sum / gain, jnp.stack([loss_sum, jnp.sum(keep)])])
        sums = plane.sum_direct(sums)
        grad_gain = sums[:-2]
        inner = jnp.sum(normed_grad * gain[None, :] * x.astype(F32), axis=1)
        sums = rows.sum_direct(jnp.concatenate([inner, sums[-2:]]))
        inner = sums[:-2]
        loss_value = sums[-2] / (sums[-1] / n_plane)

        inv_own = inv_all[:block]
        grad_input = (
            resid_grad[:block].astype(F32)
            + gain[None, :] * normed_grad
            - x.astype(F32) * (inv_own * inv_own * inner / features)[:, None]
        )
        return (
            loss_value,
            grad_gain,
            found["gate"],
            found["up"],
            found["down"],
            found["proj"],
            grad_input,
        )

    return body


def solution(mesh):
    in_specs = (
        P(PLANE, "row"),
        P("row"),
        P("row", PLANE),
        P("row", PLANE),
        P(PLANE, "row"),
        P("row", PLANE),
        P(("row", "col", "section"), None),
        P("row"),
    )
    out_specs = (
        P(),
        P("row"),
        P("row", PLANE),
        P("row", PLANE),
        P(PLANE, "row"),
        P("row", PLANE),
        P(PLANE, "row"),
    )
    body = make_body(mesh.shape["row"], mesh.shape["col"] * mesh.shape["section"])
    return jax.shard_map(body, mesh=mesh, in_specs=in_specs, out_specs=out_specs, check_vma=False)
```

```python
import functools

import jax
import jax.numpy as jnp
from jax import lax
from jax.experimental import pallas as pl
from jax.experimental.pallas import tpu as pltpu
from jax.sharding import PartitionSpec as P

PLANE = ("col", "section")
F32 = jnp.float32
BF16 = jnp.bfloat16


def mm(left, right):
    return jnp.dot(left, right, preferred_element_type=F32)


def mm_t(left, right):
    return lax.dot_general(left, right, (((1,), (1,)), ((), ())), preferred_element_type=F32)


def grad_kernel(places, n_inputs, tile, *refs):
    pieces, out_ref = refs[: len(places)], refs[n_inputs]
    left, right, sems = refs[-3:]

    @pl.when(pl.program_id(0) == 0)
    def load():
        copies = []
        for i, (piece, (side, row, column)) in enumerate(zip(pieces, places)):
            to = (left, right)[side].at[pl.ds(row, piece.shape[0]), pl.ds(column, piece.shape[1])]
            copies.append(pltpu.make_async_copy(piece, to, sems.at[i]))
        for copy in copies:
            copy.start()
        for copy in copies:
            copy.wait()

    columns = pl.ds(pl.multiple_of(pl.program_id(0) * tile, tile), tile)
    out_ref[...] = lax.dot_general(
        left[:, columns], right[...], (((0,), (0,)), ((), ())), preferred_element_type=F32
    )


def weight_grad(lefts, rights, through, *earlier):
    places, pieces, shapes = [], [], []
    for side, grid in enumerate((lefts, rights)):
        row = 0
        for line in grid:
            column = 0
            for piece in line:
                places.append((side, row, column))
                pieces.append(piece)
                column += piece.shape[1]
            row += line[0].shape[0]
        shapes.append((row, column))
    (depth, m), (_, n) = shapes
    tile = next(t for t in (512, 256, 128) if m % t == 0)
    operands = pieces + list(earlier) + list(through)
    first = len(operands) - len(through)
    made, *through = pl.pallas_call(
        functools.partial(grad_kernel, places, len(operands), tile),
        grid=(m // tile,),
        in_specs=[pl.BlockSpec(memory_space=pl.ANY)] * len(operands),
        out_specs=[pl.BlockSpec((tile, n), lambda i: (i, 0))]
        + [pl.BlockSpec(memory_space=pl.ANY)] * len(through),
        out_shape=[jax.ShapeDtypeStruct((m, n), F32)]
        + [jax.ShapeDtypeStruct(a.shape, a.dtype) for a in through],
        input_output_aliases={first + i: 1 + i for i in range(len(through))},
        scratch_shapes=[
            pltpu.VMEM((depth, m), BF16),
            pltpu.VMEM((depth, n), BF16),
            pltpu.SemaphoreType.DMA((len(pieces),)),
        ],
        compiler_params=pltpu.CompilerParams(vmem_limit_bytes=16 << 20),
        cost_estimate=pl.CostEstimate(
            flops=2 * depth * m * n,
            bytes_accessed=2 * depth * (m + n) + 4 * m * n,
            transcendentals=0,
        ),
    )(*operands)
    return made, through


def reverse_bits(value, width):
    out = 0
    for bit in range(width):
        out |= ((value >> bit) & 1) << (width - 1 - bit)
    return out


def after(value, earlier):
    first = earlier[(0,) * earlier.ndim]
    return jnp.where(first == first, value, jnp.zeros_like(value))


def halves(size):
    middle = -(-size // 256) * 128
    return [(0, middle), (middle, size)]


class Plane:
    def __init__(self, size):
        self.size = size
        self.width = (size // 2).bit_length() - 1
        assert 2 << self.width == size
        self.rev = [reverse_bits(k, self.width) for k in range(size // 2)]
        self.perms = []
        for step in range(self.width):
            even, odd = 2 << step, 2 << (self.width - 1 - step)
            self.perms.append([(c, c ^ (odd if c & 1 else even)) for c in range(size)])
        self.swap = [(c, c ^ 1) for c in range(size)]

    def gather(self, block, paired=False):
        own = block
        for perm in self.perms[1:] if paired else self.perms:
            own = jnp.concatenate([own, lax.ppermute(own, PLANE, perm)], axis=0)
        return own, lax.ppermute(own, PLANE, self.swap)

    def scatter(self, full, beside=(), paired=False):
        b = full.shape[0] // self.size
        block = lambda i: full[i * b : (i + 1) * b]
        half = self.size // 2
        mine = jnp.concatenate([block(2 * k) for k in range(half)], axis=0)
        send = jnp.concatenate([block(2 * self.rev[k] + 1) for k in range(half)], axis=0)
        got = lax.ppermute(send, PLANE, self.swap)
        acc = mine.astype(F32) + got.astype(F32)
        for i, perm in enumerate(reversed(self.perms)):
            if paired and i == len(self.perms) - 1:
                sent = acc.astype(full.dtype)
                got = lax.ppermute(sent, PLANE, perm)
                middle = acc.shape[0] // 2
                got = jnp.concatenate([got[middle:], got[:middle]], axis=0)
                return sent.astype(F32) + got.astype(F32)
            half = acc.shape[0] // 2
            kept, sent = acc[:half], acc[half:].astype(full.dtype)
            got = lax.ppermute(sent, PLANE, perm)
            if i < len(beside):
                (kept,) = beside[i]([kept], sent)
            acc = kept + got.astype(F32)
        return acc

    def sum_direct(self, value):
        value = value + lax.ppermute(value, PLANE, self.swap)
        total = value
        for chip in range(2, self.size, 2):
            perm = [(c, c ^ chip) for c in range(self.size)]
            total = total + lax.ppermute(value, PLANE, perm)
        return total


class Rows:
    def __init__(self, size, plane):
        self.size = size
        self.ring = [(r, (r + 1) % size) for r in range(size)]
        self.me = lax.axis_index("row")
        c = lax.axis_index(PLANE)
        self.odd = (c & 1) == 1
        self.slots = []
        for back in range(size):
            k = (c >> 1) ^ lax.rem(self.me + (size - back), size)
            flipped = jnp.asarray(plane.rev, jnp.int32)[k]
            self.slots.append((jnp.where(self.odd, flipped, k), jnp.where(self.odd, k, flipped)))

    def parts(self, own, other):
        b = own.shape[0] // self.size
        return [
            [
                lax.dynamic_slice_in_dim(own, at * b, b, 0),
                lax.dynamic_slice_in_dim(other, at_other * b, b, 0),
            ]
            for at, at_other in self.slots
        ]

    def place(self, full, block, back):
        rows = block.shape[0]
        return lax.dynamic_update_slice_in_dim(full, block, self.slots[back][0] * rows, 0)

    def shift(self, value):
        return lax.ppermute(value, "row", self.ring)

    def reduce(self, parts, products, beside=None):
        got, arrived = None, []
        for back in range(1, self.size + 1):
            rows = jnp.concatenate(parts[back % self.size], axis=0)
            sums = [product(rows) for product in products]
            if back == 2 and beside is not None:
                (sums[-1],) = beside([sums[-1]], sent[-1])
            if got is not None:
                sums = [s + g.astype(F32) for s, g in zip(sums, got)]
            if back < self.size:
                sent = [s.astype(BF16) for s in sums]
                got = [self.shift(s) for s in sent]
                arrived.append(got)
        return sums, arrived

    def gather(self, blocks, product):
        steps = [blocks]
        for back in range(1, self.size):
            steps.append([self.shift(b) for b in steps[-1]])
        made = [product(step) for step in steps]
        return steps, made, self.placed(made)

    def placed(self, blocks):
        out = jnp.zeros((blocks[0].shape[0] * self.size,) + blocks[0].shape[1:], blocks[0].dtype)
        for back, block in enumerate(blocks):
            out = self.place(out, block, back)
        return out

    def sum_direct(self, value):
        total = value
        for step in range(1, self.size):
            total = total + lax.ppermute(
                value, "row", [(r, r ^ step) for r in range(self.size)]
            )
        return total

    def own_order(self, value):
        half = value.shape[0] // 2
        return jnp.where(self.odd, jnp.concatenate([value[half:], value[:half]], axis=0), value)


def lines(parts):
    return [[piece] for part in parts for piece in part]


def make_body(n_row, n_plane):
    plane = Plane(n_plane)
    assert n_plane == 2 * n_row

    def body(x, gain, gate_w, up_w, down_w, proj_w, teacher, loss_mask):
        rows = Rows(n_row, plane)
        block = x.shape[0]
        features = x.shape[1] * n_row

        own, other = plane.gather((x.astype(F32) * gain[None, :]).astype(BF16))
        scaled = rows.parts(own, other)
        (gate, up), moved = rows.reduce(scaled, [lambda a: mm(a, gate_w), lambda a: mm(a, up_w)])
        squares = [jnp.sum(jnp.square(p.astype(F32) / gain[None, :]), axis=1) for p in (own, other)]
        squares = rows.sum_direct(after(jnp.concatenate(squares), moved[1][0]))
        inv_all = lax.rsqrt(squares / features + 1e-05)
        inv = jnp.concatenate(rows.parts(*jnp.split(inv_all, 2))[0])[:, None]

        target = lax.all_to_all(
            after(teacher, moved[0][0]), PLANE, split_axis=1, concat_axis=0, tiled=True
        )
        target = rows.own_order(target).astype(F32)
        keep = rows.own_order(loss_mask.astype(F32))
        inv = after(inv, target)
        gate, up = gate * inv, up * inv
        sigma = jax.nn.sigmoid(gate)
        activated = gate * sigma
        hidden = (activated * up).astype(BF16)
        cuts = halves(hidden.shape[1])
        hiddens, _, ffn = rows.gather(
            [hidden[:, lo:hi] for lo, hi in cuts],
            lambda bs: sum(mm(b, down_w[lo:hi]) for b, (lo, hi) in zip(bs, cuts)).astype(BF16),
        )
        x_other = own[block : 2 * block].astype(F32) / gain[None, :]
        x_pair = jnp.concatenate([x.astype(F32), x_other], axis=0)
        residual = (x_pair + plane.scatter(ffn, paired=True)).astype(BF16)
        residuals = rows.parts(*plane.gather(residual, paired=True))

        ecuts = halves(proj_w.shape[1])
        predicted, _ = rows.reduce(
            residuals, [lambda a, lo=lo, hi=hi: mm(a, proj_w[:, lo:hi]) for lo, hi in ecuts]
        )
        error = [p - target[:, lo:hi] for p, (lo, hi) in zip(predicted, ecuts)]
        masked = [e * keep[:, None] for e in error]

        pred_grads, _, back = rows.gather(
            [m.astype(BF16) for m in masked],
            lambda bs: sum(mm_t(b, proj_w[:, lo:hi]) for b, (lo, hi) in zip(bs, ecuts)).astype(BF16),
        )
        found = {}

        def grad(name, lefts, rights, through, *earlier):
            found[name], through = weight_grad(lefts, rights, through, *earlier)
            return through

        resid_grad = plane.scatter(
            back,
            [lambda kept, sent: grad("proj", lines(residuals), pred_grads, kept, sent)],
            paired=True,
        ).astype(BF16)
        resid_grads = rows.parts(*plane.gather(resid_grad, paired=True))

        hid_grad, _ = rows.reduce(
            resid_grads,
            [lambda a, lo=lo, hi=hi: mm_t(a, down_w[lo:hi]) for lo, hi in cuts],
            lambda own, sent: grad("down", hiddens, lines(resid_grads), own, sent),
        )
        hid_grad = jnp.concatenate(hid_grad, axis=1)
        gate_grad = hid_grad * up * (sigma * (1.0 + gate * (1.0 - sigma)))
        up_grad = hid_grad * activated
        blocks = [(gate_grad * inv).astype(BF16), (up_grad * inv).astype(BF16)]

        grads, made, back = rows.gather(
            blocks,
            lambda b: (mm_t(b[0], gate_w) + mm_t(b[1], up_w)).astype(BF16),
        )
        gates, ups = [g[:1] for g in grads], [g[1:] for g in grads]
        loss_sum = 0.5 * sum(jnp.sum(m * e) for m, e in zip(masked, error))
        gain_sum = sum(
            jnp.sum(m.astype(F32) * jnp.concatenate(p, axis=0).astype(F32), axis=0)
            for m, p in zip(made, scaled)
        )
        normed_grad = plane.scatter(
            back,
            [
                lambda kept, sent: grad("gate", lines(scaled), gates, kept, sent),
                lambda kept, sent: grad("up", lines(scaled), ups, kept, sent),
            ],
        )
        sums = jnp.concatenate([gain_sum / gain, jnp.stack([loss_sum, jnp.sum(keep)])])
        sums = plane.sum_direct(sums)
        grad_gain = sums[:-2]
        inner = jnp.sum(normed_grad * gain[None, :] * x.astype(F32), axis=1)
        sums = rows.sum_direct(jnp.concatenate([inner, sums[-2:]]))
        inner = sums[:-2]
        loss_value = sums[-2] / (sums[-1] / n_plane)

        inv_own = inv_all[:block]
        grad_input = (
            resid_grad[:block].astype(F32)
            + gain[None, :] * normed_grad
            - x.astype(F32) * (inv_own * inv_own * inner / features)[:, None]
        )
        return (
            loss_value,
            grad_gain,
            found["gate"],
            found["up"],
            found["down"],
            found["proj"],
            grad_input,
        )

    return body


def solution(mesh):
    in_specs = (
        P(PLANE, "row"),
        P("row"),
        P("row", PLANE),
        P("row", PLANE),
        P(PLANE, "row"),
        P("row", PLANE),
        P(("row", "col", "section"), None),
        P("row"),
    )
    out_specs = (
        P(),
        P("row"),
        P("row", PLANE),
        P("row", PLANE),
        P(PLANE, "row"),
        P("row", PLANE),
        P(PLANE, "row"),
    )
    body = make_body(mesh.shape["row"], mesh.shape["col"] * mesh.shape["section"])
    return jax.shard_map(body, mesh=mesh, in_specs=in_specs, out_specs=out_specs, check_vma=False)
```
